128 devices in a mesh: seq: 64 (over y_lo, x, z, core), head: 2 (over y_hi).
Axes of the slice: x: 4, y: 4 (y_hi: 2, y_lo: 2; y = y_hi * 2 + y_lo), z: 4, core: 2. Of those that a mesh axis runs over, the one named last changes fastest.
Arguments:
- ctx_hidden: bfloat16 [32768, 5120], P('seq', 'head'), may hold values from -1200 to 1200
- fin_hidden: bfloat16 [1024, 5120], P('seq', 'head'), may hold values from -1200 to 1200
- lengths: int32 [64], replicated, may hold values from 1 to 512, 24576 in all
- ln_gain: float32 [5120], P('head'), may hold values from 0.1 to 1.9
- q_weight: bfloat16 [5120, 2560], P(None, 'head'), may hold values from -0.078125 to 0.078125
- k_weight: bfloat16 [5120, 512], P(None, 'head'), may hold values from -0.078125 to 0.078125
- v_weight: bfloat16 [5120, 512], P(None, 'head'), may hold values from -0.078125 to 0.078125
- q_gain: float32 [128], replicated, may hold values from 1.2 to 13.2
- k_gain: float32 [128], replicated, may hold values from 1.2 to 13.2
Outputs:
- ctx_out: bfloat16 [32768, 2560], P('seq', 'head')
- fin_out: bfloat16 [1024, 2560], P('seq', 'head')
The draws below stay inside these ranges and needn't reach their ends.
Inputs may be any that keep to these rules, and one draw needn't show every extreme that they name: lengths[b] counts the live rows at the start of context block b; the rest of the block is padding; the blocks hold 24576 live tokens together.
All inputs are finite; a program needn't handle non-finite values.
Results may differ from the reference program's by a relative error of at most 0.012.
The reference program's roundings to bfloat16 on the way (of `ctx_norm` and `fin_norm`) count: a program that leaves them out, or rounds other values in their place, can miss the bound.
Values may be sent and summed in bfloat16 or wider, within the bound.
No kernel may reach another device: no remote copies, remote signals or barrier semaphores. Data moves between devices by JAX's collectives and lax.ppermute only.
A program may use at most 192 MiB of HBM per device.

```python
import math
import jax
import jax.numpy as jnp
import numpy as np
from jax import lax

D = 5120
HD = 128
GROUP = 5
KV_HEADS = 4
CTX_DEV = 512
FIN_DEV = 16
QH = 20
CTX_ROWS = 32768
FIN_ROWS = 1024
LIVE = 24576
N_SEQ = 64


def column_scales(key):
    shared_key = jax.random.fold_in(key, 101)
    spread = jnp.exp(jnp.log(10.0) * jax.random.uniform(shared_key, (D,), jnp.float32))
    column_ramp = jnp.exp(jnp.log(3.0) * jnp.arange(D, dtype=jnp.float32) / D)
    return spread * column_ramp


def draw_ctx_hidden(key, part):
    columns = column_scales(key)
    key = jax.random.fold_in(key, 11)
    first_key, second_key = jax.random.split(key, 2)
    noise_draw = jnp.clip(jax.random.normal(first_key, (CTX_ROWS, D), jnp.float32), -4.0, 4.0)
    row_factor = jnp.exp(jnp.log(10.0) * jax.random.uniform(second_key, (CTX_ROWS, 1), jnp.float32))
    values = row_factor * noise_draw * columns
    return values.astype(jnp.bfloat16)


def draw_fin_hidden(key, part):
    columns = column_scales(key)
    key = jax.random.fold_in(key, 12)
    first_key, second_key = jax.random.split(key, 2)
    noise_draw = jnp.clip(jax.random.normal(first_key, (FIN_ROWS, D), jnp.float32), -4.0, 4.0)
    row_factor = jnp.exp(jnp.log(10.0) * jax.random.uniform(second_key, (FIN_ROWS, 1), jnp.float32))
    values = row_factor * noise_draw * columns
    return values.astype(jnp.bfloat16)


def draw_q_gain(key, part):
    key = jax.random.fold_in(key, 21)
    base_gain = 1.2 * jnp.exp(jnp.log(2.0) * jax.random.uniform(key, (HD,), jnp.float32))
    return base_gain.astype(jnp.float32)


def draw_k_gain(key, part):
    key = jax.random.fold_in(key, 22)
    base_gain = 1.2 * jnp.exp(jnp.log(2.0) * jax.random.uniform(key, (HD,), jnp.float32))
    return base_gain.astype(jnp.float32)


def block_scale(rng, extent, shards, smallest, high):
    level, own = 1.0, jax.random.fold_in(rng, 6)
    for axis_at, parts in shards:
        heights = jnp.exp(jax.random.uniform(jax.random.fold_in(own, axis_at), (parts,), jnp.float32, smallest / len(shards), high / len(shards)))
        level = level * jnp.repeat(heights, extent[axis_at] // parts).reshape([-1 if axis == axis_at else 1 for axis in range(len(extent))])
    return level


def split_up(amount, total, most, lean):
    loads = [(1 << 20) // math.isqrt(grade ** lean) + 1 for grade in range(2, amount + 1)]
    surplus, holding = total - most - (amount - 1), [1] * (amount - 1)
    while surplus > 0:
        candidates = [i for i in range(amount - 1) if holding[i] < most]
        pool, budget = sum([loads[i] for i in candidates]), surplus
        for i in candidates:
            extra = min(most - holding[i], max(1, budget * loads[i] // pool), surplus)
            holding[i] = holding[i] + extra
            surplus = surplus - extra
    return np.array([most] + holding)


def uneven(rng, amount, total, most, skew):
    if amount == 2:
        one = jax.random.randint(rng, (), max(1, total - most), min(most, total - 1) + 1)
        return jnp.stack([one, total - one])
    sizes = jnp.asarray(split_up(amount, total, most, skew), jnp.int32)
    twos = (amount - 1) // 2
    donor, receiver = sizes[1:1 + 2 * twos:2], sizes[2:2 + 2 * twos:2]
    margin = jnp.minimum(donor - 1, most - receiver)
    moved = jax.random.randint(jax.random.fold_in(rng, 1), (twos,), 0, 1 << 20) % (margin + 1)
    sizes = sizes.at[1:1 + 2 * twos:2].set(donor - moved).at[2:2 + 2 * twos:2].set(receiver + moved)
    return sizes[jax.random.permutation(jax.random.fold_in(rng, 2), amount)]


def bell_draw(stream_key, extent, width, reach, pieces=(), kind=jnp.bfloat16):
    entries = jax.random.normal(stream_key, extent, jnp.float32) * width
    if len(pieces) > 0:
        entries = block_scale(stream_key, extent, pieces, -0.22, 0.18) * entries
    return jnp.clip(entries, min=-reach, max=reach).astype(kind)


def setup_inputs(seed: int = 0) -> dict:
    arg_keys = jax.random.split(jax.random.key(seed), 10)
    ctx_hidden = draw_ctx_hidden(jax.random.fold_in(arg_keys[9], 71), 0)
    fin_hidden = draw_fin_hidden(jax.random.fold_in(arg_keys[9], 71), 0)
    lengths = uneven(arg_keys[2], N_SEQ, LIVE, CTX_DEV, 2).astype(jnp.int32)
    ln_gain = jnp.clip(1.0 + 0.18 * jax.random.normal(arg_keys[3], (D,), jnp.float32), 0.1, 1.9)
    q_weight = bell_draw(arg_keys[4], (D, QH * HD), D ** -0.5, 0.078125, ((1, 2),))
    k_weight = bell_draw(arg_keys[5], (D, KV_HEADS * HD), D ** -0.5, 0.078125, ((1, 2),))
    v_weight = bell_draw(arg_keys[6], (D, KV_HEADS * HD), D ** -0.5, 0.078125, ((1, 2),))
    q_gain = draw_q_gain(jax.random.fold_in(arg_keys[9], 71), 0)
    k_gain = draw_k_gain(jax.random.fold_in(arg_keys[9], 71), 0)
    return dict(ctx_hidden=ctx_hidden, fin_hidden=fin_hidden, lengths=lengths, ln_gain=ln_gain, q_weight=q_weight, k_weight=k_weight, v_weight=v_weight, q_gain=q_gain, k_gain=k_gain)


eps_norm = 1e-06
rope_base = 1000000.0
masked_score = -1e+30

def half_round(values):
    return lax.optimization_barrier(values.astype(jnp.bfloat16))

def row_scale(values, gain_vector):
    return values * lax.rsqrt(lax.optimization_barrier(jnp.mean(values * values, axis=-1, keepdims=True)) + eps_norm) * gain_vector

def rotate(values, positions):
    half_dim = values.shape[-1] // 2
    exponent = jnp.arange(half_dim, dtype=jnp.float32) * (-2.0 / values.shape[-1])
    frequency = jnp.power(jnp.float32(rope_base), exponent)
    angles = positions.astype(jnp.float32)[:, None] * frequency[None, :]
    angles = jnp.concatenate([angles, angles], axis=-1)[:, None, :]
    turned = jnp.concatenate([-values[..., half_dim:], values[..., :half_dim]], axis=-1)
    return values * jnp.cos(angles) + turned * jnp.sin(angles)

def project_heads(normed, weight, gain_vector, positions):
    raw_proj = jnp.dot(normed, weight, preferred_element_type=jnp.float32)
    raw_proj = raw_proj.reshape(normed.shape[0], weight.shape[1] // HD, HD)
    return half_round(rotate(row_scale(raw_proj, gain_vector), positions))

def project_values(normed, weight):
    value_proj = jnp.dot(normed, weight, preferred_element_type=jnp.float32)
    return half_round(value_proj).reshape(normed.shape[0], weight.shape[1] // HD, HD)

def reference(ctx_hidden, fin_hidden, lengths, ln_gain, q_weight, k_weight, v_weight, q_gain, k_gain):
    ctx_norm = half_round(row_scale(ctx_hidden.astype(jnp.float32), ln_gain))
    fin_norm = half_round(row_scale(fin_hidden.astype(jnp.float32), ln_gain))
    starts = (jnp.cumsum(lengths) - lengths).astype(jnp.int32)
    live_total = jnp.sum(lengths).astype(jnp.int32)
    block_rows = jnp.arange(CTX_DEV, dtype=jnp.int32)
    ctx_pos = (starts[:, None] + block_rows[None, :]).reshape(-1)
    fin_pos = live_total + jnp.arange(FIN_ROWS, dtype=jnp.int32)
    q_ctx = project_heads(ctx_norm, q_weight, q_gain, ctx_pos)
    k_ctx = project_heads(ctx_norm, k_weight, k_gain, ctx_pos)
    v_ctx = project_values(ctx_norm, v_weight)
    q_fin = project_heads(fin_norm, q_weight, q_gain, fin_pos)
    k_fin = project_heads(fin_norm, k_weight, k_gain, fin_pos)
    v_fin = project_values(fin_norm, v_weight)
    score_scale = HD ** (-0.5)
    q_blocks = q_ctx.reshape(N_SEQ, CTX_DEV, KV_HEADS, GROUP, HD)
    k_blocks = k_ctx.reshape(N_SEQ, CTX_DEV, KV_HEADS, HD)
    v_blocks = v_ctx.reshape(N_SEQ, CTX_DEV, KV_HEADS, HD)
    anchor_keys = k_blocks[0]
    anchor_values = v_blocks[0]
    anchor_mask = block_rows < lengths[0]
    causal = block_rows[None, :] <= block_rows[:, None]

    def encode(block_item):
        query_rows, own_key, own_value, own_length, block_id = block_item
        key_rows = jnp.concatenate([anchor_keys, own_key], axis=0).astype(jnp.float32)
        value_rows = jnp.concatenate([anchor_values, own_value], axis=0).astype(jnp.float32)
        scores = jnp.einsum('rkgd,skd->kgrs', query_rows.astype(jnp.float32), key_rows) * score_scale
        anchor_open = jnp.broadcast_to((anchor_mask & (block_id > 0))[None, :], (CTX_DEV, CTX_DEV))
        allowed = jnp.concatenate([anchor_open, causal], axis=1)
        scores = jnp.where(allowed, scores, masked_score)
        row_peak = lax.optimization_barrier(jnp.max(scores, axis=-1, keepdims=True))
        weights = jnp.where(allowed, jnp.exp(scores - row_peak), 0.0)
        denominator = lax.optimization_barrier(jnp.sum(weights, axis=-1))
        mixed_rows = jnp.einsum('kgrs,skd->rkgd', half_round(weights).astype(jnp.float32), value_rows)
        mixed_rows = mixed_rows / jnp.transpose(denominator, (2, 0, 1))[..., None]
        mixed_rows = jnp.where((block_rows < own_length)[:, None, None, None], mixed_rows, 0.0)
        return mixed_rows.astype(jnp.bfloat16).reshape(CTX_DEV, KV_HEADS * GROUP * HD)
    ctx_out = lax.map(encode, (q_blocks, k_blocks, v_blocks, lengths, jnp.arange(N_SEQ, dtype=jnp.int32)))
    ctx_out = ctx_out.reshape(CTX_ROWS, KV_HEADS * GROUP * HD)
    query_all = q_fin.reshape(FIN_ROWS, KV_HEADS, GROUP, HD).astype(jnp.float32)
    query_ids = jnp.arange(FIN_ROWS, dtype=jnp.int32)
    key_ids = jnp.arange(CTX_DEV + FIN_DEV, dtype=jnp.int32)
    kf_blocks = k_fin.reshape(N_SEQ, FIN_DEV, KV_HEADS, HD)
    vf_blocks = v_fin.reshape(N_SEQ, FIN_DEV, KV_HEADS, HD)

    def absorb(running, block_item):
        run_peak, run_denominator, run_mixed = running
        own_key, own_value, fin_key, fin_value, own_length, block_id = block_item
        key_rows = jnp.concatenate([own_key, fin_key], axis=0).astype(jnp.float32)
        value_rows = jnp.concatenate([own_value, fin_value], axis=0).astype(jnp.float32)
        scores = jnp.einsum('qkgd,skd->kgqs', query_all, key_rows) * score_scale
        fin_index = block_id * FIN_DEV + key_ids - CTX_DEV
        allowed = jnp.where((key_ids < CTX_DEV)[None, :], (key_ids < own_length)[None, :], fin_index[None, :] <= query_ids[:, None])
        scores = jnp.where(allowed, scores, masked_score)
        row_peak = lax.optimization_barrier(jnp.max(scores, axis=-1))
        weights = jnp.where(allowed, jnp.exp(scores - row_peak[..., None]), 0.0)
        denominator = lax.optimization_barrier(jnp.sum(weights, axis=-1))
        mixed_rows = jnp.einsum('kgqs,skd->qkgd', half_round(weights).astype(jnp.float32), value_rows)
        new_peak = jnp.maximum(run_peak, row_peak)
        old_factor = jnp.exp(run_peak - new_peak)
        new_factor = jnp.exp(row_peak - new_peak)
        run_denominator = run_denominator * old_factor + denominator * new_factor
        run_mixed = run_mixed * jnp.transpose(old_factor, (2, 0, 1))[..., None] + mixed_rows * jnp.transpose(new_factor, (2, 0, 1))[..., None]
        return ((new_peak, run_denominator, run_mixed), None)
    start_state = (jnp.full((KV_HEADS, GROUP, FIN_ROWS), masked_score, jnp.float32), jnp.zeros((KV_HEADS, GROUP, FIN_ROWS), jnp.float32), jnp.zeros((FIN_ROWS, KV_HEADS, GROUP, HD), jnp.float32))
    final_state, unused_out = lax.scan(absorb, start_state, (k_blocks, v_blocks, kf_blocks, vf_blocks, lengths, jnp.arange(N_SEQ, dtype=jnp.int32)))
    final_peak, final_denominator, final_mixed = final_state
    fin_out = final_mixed / jnp.transpose(final_denominator, (2, 0, 1))[..., None]
    fin_out = fin_out.astype(jnp.bfloat16).reshape(FIN_ROWS, KV_HEADS * GROUP * HD)
    return (ctx_out, fin_out)
```

```python
import functools

import jax
import jax.numpy as jnp
from jax import lax
from jax.experimental import pallas as pl
from jax.experimental.pallas import tpu as pltpu
from jax.sharding import PartitionSpec as P

HD = 128
GROUP = 5
KVH = 2
QH = 10
eps_norm = 1e-06
rope_base = 1000000.0
masked_score = -1e30
log2e = 1.4426950408889634
score_factor = HD ** (-0.5) * log2e
CHUNK = 128
PAD = 128
F32 = jnp.float32
BF = jnp.bfloat16
NT = (((1,), (1,)), ((), ()))
SWAP = [(0, 1), (1, 0)]


def number(l, x, z, c):
    return ((l * 4 + x) * 4 + z) * 2 + c


def coords(s):
    return s // 32, s // 8 % 4, s // 2 % 4, s % 2


def route(move):
    return [(s, number(*move(*coords(s)))) for s in range(64)]


def to_z(k):
    return route(lambda l, x, z, c: (l, x, (z + k) % 4, c))


def to_x(k):
    return route(lambda l, x, z, c: (l, (x + k) % 4, z, c))


TO_Y = route(lambda l, x, z, c: (1 - l, x, z, c))
TO_CORE = route(lambda l, x, z, c: (l, x, z, 1 - c))


def project_kernel(
    place, own, other, gain_own, gain_other, q_gain, k_gain, cos, sin, wq, wk, wv,
    q_out, k_out, v_out, normed, weights, sems,
):
    rows, half = own.shape
    copies = []
    for n in range(7):
        if n < 5:
            source = wq.at[:, pl.ds(n * 256, 256)]
        else:
            source = wk if n == 5 else wv
        copies.append(pltpu.make_async_copy(source, weights.at[n], sems.at[n]))
        copies[-1].start()
    mine = pl.multiple_of(place[0] * half, half)
    theirs = pl.multiple_of((1 - place[0]) * half, half)

    @pl.loop(0, rows // 16)
    def _(step):
        at = pl.ds(pl.multiple_of(step * 16, 16), 16)
        a = own[at, :].astype(F32)
        b = other[at, :].astype(F32)
        total = jnp.sum(a * a, axis=1, keepdims=True) + jnp.sum(b * b, axis=1, keepdims=True)
        scale = lax.rsqrt(total / (2 * half) + eps_norm)
        normed[at, pl.ds(mine, half)] = (a * scale * gain_own[...]).astype(BF)
        normed[at, pl.ds(theirs, half)] = (b * scale * gain_other[...]).astype(BF)

    for n in range(7):
        copies[n].wait()
        raw = jnp.dot(normed[...], weights[n], preferred_element_type=F32)
        for part in range(2):
            piece = raw[:, part * HD:(part + 1) * HD]
            if n == 6:
                v_out[:, part * HD:(part + 1) * HD] = piece.astype(BF)
                continue
            gain = q_gain if n < 5 else k_gain
            mean = jnp.sum(piece * piece, axis=1, keepdims=True) * (1.0 / HD)
            piece = piece * lax.rsqrt(mean + eps_norm) * gain[...]
            turned = pltpu.roll(piece, HD // 2, 1)
            piece = (piece * cos[...] + turned * sin[...]).astype(BF)
            if n < 5:
                q_out[:, n * 256 + part * HD:n * 256 + (part + 1) * HD] = piece
            else:
                k_out[:, part * HD:(part + 1) * HD] = piece


VMEM = pl.BlockSpec(memory_space=pltpu.VMEM)
SMEM = pl.BlockSpec(memory_space=pltpu.SMEM)
ANY = pl.BlockSpec(memory_space=pl.ANY)


def project(place, own, other, gains, q_gain, k_gain, turn, weights):
    rows, half = own.shape
    return pl.pallas_call(
        project_kernel,
        out_shape=(
            jax.ShapeDtypeStruct((rows, QH * HD), BF),
            jax.ShapeDtypeStruct((rows, KVH * HD), BF),
            jax.ShapeDtypeStruct((rows, KVH * HD), BF),
        ),
        in_specs=[SMEM] + [VMEM] * 8 + [ANY] * 3,
        out_specs=(VMEM, VMEM, VMEM),
        scratch_shapes=[
            pltpu.VMEM((rows, 2 * half), BF),
            pltpu.VMEM((7, 2 * half, 256), BF),
            pltpu.SemaphoreType.DMA((7,)),
        ],
        compiler_params=pltpu.CompilerParams(vmem_limit_bytes=36 << 20),
        cost_estimate=pl.CostEstimate(
            flops=2 * rows * 5120 * 1792, bytes_accessed=5120 * 1792 * 2, transcendentals=0
        ),
    )(place, own, other, *gains, q_gain, k_gain, *turn, *weights)


def ctx_kernel(first, info, q, ka, va, ko, vo, out):
    rows = q.shape[0]
    keys = first + rows
    position, own_length, anchor_length = info[0], info[1], info[2]
    limit = jnp.where(position > 0, anchor_length, 0)
    s1 = lax.dot_general(q[...], ka[...], NT, preferred_element_type=F32) * score_factor
    s2 = lax.dot_general(q[...], ko[:keys, :], NT, preferred_element_type=F32) * score_factor
    s1 = jnp.where(lax.broadcasted_iota(jnp.int32, s1.shape, 1) < limit, s1, masked_score)
    row = lax.broadcasted_iota(jnp.int32, s2.shape, 0) + first
    s2 = jnp.where(lax.broadcasted_iota(jnp.int32, s2.shape, 1) <= row, s2, masked_score)
    peak = jnp.maximum(
        jnp.max(s1, axis=1, keepdims=True), jnp.max(s2, axis=1, keepdims=True)
    )
    p1 = jnp.exp2(s1 - peak)
    p2 = jnp.exp2(s2 - peak)
    total = jnp.sum(p1, axis=1, keepdims=True) + jnp.sum(p2, axis=1, keepdims=True)
    mixed = jnp.dot(p1.astype(BF), va[...], preferred_element_type=F32)
    mixed += jnp.dot(p2.astype(BF), vo[:keys, :], preferred_element_type=F32)
    mixed = mixed / total
    row = lax.broadcasted_iota(jnp.int32, mixed.shape, 0) + first
    out[...] = jnp.where(row < own_length, mixed, 0.0).astype(BF)


def ctx_attention(first, info, q, anchor, k, v):
    rows = q.shape[0]
    count = k.shape[0]
    return pl.pallas_call(
        functools.partial(ctx_kernel, first),
        grid=(QH,),
        out_shape=jax.ShapeDtypeStruct((rows, QH * HD), BF),
        in_specs=[
            SMEM,
            pl.BlockSpec((rows, HD), lambda h: (0, h)),
            pl.BlockSpec((count, HD), lambda h: (0, h // GROUP)),
            pl.BlockSpec((count, HD), lambda h: (0, KVH + h // GROUP)),
            pl.BlockSpec((count, HD), lambda h: (0, h // GROUP)),
            pl.BlockSpec((count, HD), lambda h: (0, h // GROUP)),
        ],
        out_specs=pl.BlockSpec((rows, HD), lambda h: (0, h)),
        compiler_params=pltpu.CompilerParams(vmem_limit_bytes=32 << 20),
        cost_estimate=pl.CostEstimate(
            flops=4 * rows * (first + rows + count) * QH * HD,
            bytes_accessed=4 * rows * QH * HD,
            transcendentals=rows * (first + rows + count) * QH,
        ),
    )(info, q, anchor, anchor, k, v)


def put(base, lane, column, value):
    return jnp.where(lane == column, value, base)


def fin_kernel(info, ids, q, k, v, kf, vf, out):
    rows = q.shape[0]
    count = k.shape[0]
    position, own_length, fin_count = info[0], info[1], info[3]
    lane = lax.broadcasted_iota(jnp.int32, (rows, HD), 1)
    fin_open = (lane < fin_count) & (lane + position * fin_count <= ids[...])
    ctx_open = lax.broadcasted_iota(jnp.int32, (rows, count), 1) < own_length
    stats = jnp.zeros((rows, HD), F32)
    for h in range(QH):
        g = h // GROUP
        here, there = slice(h * HD, (h + 1) * HD), slice(g * HD, (g + 1) * HD)
        query = q[:, here]
        s1 = lax.dot_general(query, k[:, there], NT, preferred_element_type=F32) * score_factor
        s2 = lax.dot_general(query, kf[:, there], NT, preferred_element_type=F32) * score_factor
        s1 = jnp.where(ctx_open, s1, masked_score)
        s2 = jnp.where(fin_open, s2, masked_score)
        peak = jnp.maximum(
            jnp.max(s1, axis=1, keepdims=True), jnp.max(s2, axis=1, keepdims=True)
        )
        peak = peak.astype(BF).astype(F32)
        p1 = jnp.exp2(s1 - peak)
        p2 = jnp.exp2(s2 - peak)
        total = jnp.sum(p1, axis=1, keepdims=True) + jnp.sum(p2, axis=1, keepdims=True)
        mixed = jnp.dot(p1.astype(BF), v[:, there], preferred_element_type=F32)
        mixed += jnp.dot(p2.astype(BF), vf[:, there], preferred_element_type=F32)
        out[:, here] = mixed.astype(BF)
        high = total.astype(BF).astype(F32)
        stats = put(stats, lane, h, peak)
        stats = put(stats, lane, 16 + h, high)
        stats = put(stats, lane, 32 + h, total - high)
    out[:, QH * HD:] = stats.astype(BF)


def fin_attention(info, ids, q, k, v, kf, vf):
    rows = q.shape[0]
    tile = 128
    whole = lambda i: (0, 0)
    return pl.pallas_call(
        fin_kernel,
        grid=(rows // tile,),
        out_shape=jax.ShapeDtypeStruct((rows, (QH + 1) * HD), BF),
        in_specs=[
            SMEM,
            pl.BlockSpec((tile, 1), lambda i: (i, 0)),
            pl.BlockSpec((tile, QH * HD), lambda i: (i, 0)),
            pl.BlockSpec(k.shape, whole),
            pl.BlockSpec(v.shape, whole),
            pl.BlockSpec(kf.shape, whole),
            pl.BlockSpec(vf.shape, whole),
        ],
        out_specs=pl.BlockSpec((tile, (QH + 1) * HD), lambda i: (i, 0)),
        compiler_params=pltpu.CompilerParams(vmem_limit_bytes=32 << 20),
        cost_estimate=pl.CostEstimate(
            flops=4 * rows * 640 * QH * HD, bytes_accessed=4 * rows * QH * HD,
            transcendentals=rows * 640 * QH,
        ),
    )(info, ids, q, k, v, kf, vf)


def merge_kernel(count, final, *refs):
    parts, out = refs[:count], refs[count]
    stats = [part[:, QH * HD:].astype(F32) for part in parts]
    lane = lax.broadcasted_iota(jnp.int32, stats[0].shape, 1)
    top = functools.reduce(jnp.maximum, stats)
    weights = [jnp.exp2(jnp.where(lane < QH, stat - top, 0.0)) for stat in stats]
    totals = [pltpu.roll(stat, HD - 16, 1) + pltpu.roll(stat, HD - 32, 1) for stat in stats]
    total = sum(w * t for w, t in zip(weights, totals))
    if final:
        inverse = 1.0 / jnp.where(lane < QH, total, 1.0)
        weights = [w * inverse for w in weights]
    for h in range(QH):
        here = slice(h * HD, (h + 1) * HD)
        mixed = sum(
            part[:, here].astype(F32) * w[:, h:h + 1] for part, w in zip(parts, weights)
        )
        out[:, here] = mixed.astype(BF)
    if not final:
        high = total.astype(BF).astype(F32)
        packed = jnp.where(
            lane < 16,
            top,
            jnp.where(lane < 32, pltpu.roll(high, 16, 1), pltpu.roll(total - high, 32, 1)),
        )
        packed = jnp.where(lane < 48, packed, 0.0)
        out[:, QH * HD:] = packed.astype(BF)


def merge(parts, final=False):
    rows = parts[0].shape[0]
    tile = min(rows, 64)
    width = (QH + 1) * HD
    out_width = QH * HD if final else width
    return pl.pallas_call(
        functools.partial(merge_kernel, len(parts), final),
        grid=(rows // tile,),
        out_shape=jax.ShapeDtypeStruct((rows, out_width), BF),
        in_specs=[pl.BlockSpec((tile, width), lambda i: (i, 0))] * len(parts),
        out_specs=pl.BlockSpec((tile, out_width), lambda i: (i, 0)),
        compiler_params=pltpu.CompilerParams(vmem_limit_bytes=32 << 20),
        cost_estimate=pl.CostEstimate(
            flops=4 * len(parts) * rows * width, bytes_accessed=2 * (len(parts) + 1) * rows * width,
            transcendentals=0,
        ),
    )(*parts)


def broadcast_first(value, seq):
    l, x, z, c = coords(seq)
    stages = [
        (route_from(lambda l, x, z, c: (l, x, z, c) == (0, 0, 0, 0), lambda l, x, z, c: (l, x, 2, c)),
         (l == 0) & (x == 0) & (z == 2) & (c == 0)),
        (route_from(lambda l, x, z, c: l == 0 and x == 0 and z in (0, 2) and c == 0, lambda l, x, z, c: (l, x, z + 1, c)),
         (l == 0) & (x == 0) & (z % 2 == 1) & (c == 0)),
        (route_from(lambda l, x, z, c: l == 0 and x == 0 and c == 0, lambda l, x, z, c: (l, 2, z, c)),
         (l == 0) & (x == 2) & (c == 0)),
        (route_from(lambda l, x, z, c: l == 0 and x in (0, 2) and c == 0, lambda l, x, z, c: (l, x + 1, z, c)),
         (l == 0) & (x % 2 == 1) & (c == 0)),
        (route_from(lambda l, x, z, c: l == 0 and c == 0, lambda l, x, z, c: (1, x, z, c)),
         (l == 1) & (c == 0)),
        (route_from(lambda l, x, z, c: c == 0, lambda l, x, z, c: (l, x, z, 1)), c == 1),
    ]
    for pairs, takes in stages:
        value = jnp.where(takes, lax.ppermute(value, "seq", pairs), value)
    return value


def route_from(holds, move):
    return [(s, number(*move(*coords(s)))) for s in range(64) if holds(*coords(s))]


def local(ctx_hidden, fin_hidden, lengths, ln_gain, q_weight, k_weight, v_weight, q_gain, k_gain):
    ctx_count, half = ctx_hidden.shape
    fin_count = fin_hidden.shape[0]
    head = lax.axis_index("head").astype(jnp.int32)
    seq = lax.axis_index("seq").astype(jnp.int32)
    own_gain = ln_gain.reshape(1, half)
    other_fin = lax.ppermute(fin_hidden, "head", SWAP)
    other_gain = lax.ppermute(own_gain, "head", SWAP)
    starts = range(0, ctx_count, CHUNK)
    own_rows = [ctx_hidden[i:i + CHUNK] for i in starts]
    other_rows = [lax.ppermute(rows, "head", SWAP) for rows in own_rows]

    block_ids = jnp.arange(64, dtype=jnp.int32)
    own_start = jnp.sum(jnp.where(block_ids < seq, lengths, 0))
    own_length = jnp.sum(jnp.where(block_ids == seq, lengths, 0))
    live_total = jnp.sum(lengths)
    positions = jnp.concatenate([
        own_start + jnp.arange(ctx_count, dtype=jnp.int32),
        live_total + seq * fin_count + jnp.arange(fin_count, dtype=jnp.int32),
    ])
    exponent = jnp.arange(HD // 2, dtype=F32) * (-2.0 / HD)
    frequency = jnp.power(F32(rope_base), exponent)
    angles = positions.astype(F32)[:, None] * frequency[None, :]
    cos, sin = jnp.cos(angles), jnp.sin(angles)
    cos = jnp.concatenate([cos, cos], axis=1)
    sin = jnp.concatenate([-sin, sin], axis=1)

    place = head.reshape(1)
    gains = (own_gain, other_gain)
    qg, kg = q_gain.reshape(1, HD), k_gain.reshape(1, HD)
    weights = (q_weight, k_weight, v_weight)
    q_fin, k_fin, v_fin = project(
        place, fin_hidden, other_fin, gains, qg, kg, (cos[ctx_count:], sin[ctx_count:]), weights
    )
    k_fin = jnp.pad(k_fin, ((0, PAD - fin_count), (0, 0)))
    v_fin = jnp.pad(v_fin, ((0, PAD - fin_count), (0, 0)))

    gathered = jnp.concatenate([q_fin, lax.ppermute(q_fin, "seq", TO_Y)], axis=0)
    gathered = jnp.concatenate(
        [gathered] + [lax.ppermute(gathered, "seq", to_x(-k)) for k in (1, 2, 3)], axis=0
    )
    gathered = jnp.concatenate(
        [gathered] + [lax.ppermute(gathered, "seq", to_z(-k)) for k in (1, 2, 3)], axis=0
    )
    gathered = jnp.concatenate([gathered, lax.ppermute(gathered, "seq", TO_CORE)], axis=0)
    my_l, my_x, my_z, my_c = coords(seq)
    slot = jnp.arange(64, dtype=jnp.int32)
    owner = number(
        (my_l + slot % 2) % 2, (my_x + slot // 2 % 4) % 4, (my_z + slot // 8 % 4) % 4, (my_c + slot // 32) % 2
    )
    ids = (owner[:, None] * fin_count + jnp.arange(fin_count, dtype=jnp.int32)[None, :]).reshape(-1, 1)

    made = [
        project(place, own, other, gains, qg, kg, (cos[i:i + CHUNK], sin[i:i + CHUNK]), weights)
        for i, own, other in zip(starts, own_rows, other_rows)
    ]
    k_ctx = jnp.concatenate([part[1] for part in made], axis=0)
    v_ctx = jnp.concatenate([part[2] for part in made], axis=0)
    pieces = [
        broadcast_first(jnp.concatenate([part[1], part[2]], axis=1), seq) for part in made
    ]
    anchor = jnp.concatenate(pieces, axis=0)

    info = jnp.stack([seq, own_length, lengths[0], jnp.int32(fin_count)])
    partial = fin_attention(info, ids, gathered, k_ctx, v_ctx, k_fin, v_fin)
    ctx_out = jnp.concatenate(
        [ctx_attention(i, info, part[0], anchor, k_ctx, v_ctx) for i, part in zip(starts, made)], axis=0
    )
    rows = partial.shape[0] // 2
    partial = merge([partial[:rows], lax.ppermute(partial[rows:], "seq", TO_CORE)])
    rows //= 4
    partial = merge(
        [partial[:rows]]
        + [lax.ppermute(partial[k * rows:(k + 1) * rows], "seq", to_z(k)) for k in (1, 2, 3)]
    )
    rows //= 4
    partial = merge(
        [partial[:rows]]
        + [lax.ppermute(partial[k * rows:(k + 1) * rows], "seq", to_x(k)) for k in (1, 2, 3)]
    )
    rows //= 2
    fin_out = merge([partial[:rows], lax.ppermute(partial[rows:], "seq", TO_Y)], final=True)
    return ctx_out, fin_out


def solution(mesh):
    return jax.shard_map(
        local,
        mesh=mesh,
        in_specs=(
            P("seq", "head"),
            P("seq", "head"),
            P(),
            P("head"),
            P(None, "head"),
            P(None, "head"),
            P(None, "head"),
            P(),
            P(),
        ),
        out_specs=(P("seq", "head"), P("seq", "head")),
        check_vma=False,
    )
```

```python
import functools

import jax
import jax.numpy as jnp
from jax import lax
from jax.experimental import pallas as pl
from jax.experimental.pallas import tpu as pltpu
from jax.sharding import PartitionSpec as P

HD = 128
GROUP = 5
KVH = 2
QH = 10
eps_norm = 1e-06
rope_base = 1000000.0
masked_score = -1e30
log2e = 1.4426950408889634
score_factor = HD ** (-0.5) * log2e
CHUNK = 128
F32 = jnp.float32
BF = jnp.bfloat16
NT = (((1,), (1,)), ((), ()))
SWAP = [(0, 1), (1, 0)]


def number(l, x, z, c):
    return ((l * 4 + x) * 4 + z) * 2 + c


def coords(s):
    return s // 32, s // 8 % 4, s // 2 % 4, s % 2


def route(move):
    return [(s, number(*move(*coords(s)))) for s in range(64)]


def to_z(k):
    return route(lambda l, x, z, c: (l, x, z ^ k, c))


def to_x(k):
    return route(lambda l, x, z, c: (l, x ^ k, z, c))


def both(move):
    pairs = []
    for s in range(64):
        l, x, z, c = coords(s)
        for h in range(2):
            to_l, to_h = move(l, h)
            pairs.append((2 * s + h, 2 * number(to_l, x, z, c) + to_h))
    return pairs


TO_CROSS = both(lambda l, h: (1 - l, 1 - h))
SWAP_FIRST = [(0, 1), (1, 0)]
SWAP_REST = [pair for pair in both(lambda l, h: (l, 1 - h)) if pair[0] > 1]
TO_Y = route(lambda l, x, z, c: (1 - l, x, z, c))
TO_CORE = route(lambda l, x, z, c: (l, x, z, 1 - c))


VMEM = pl.BlockSpec(memory_space=pltpu.VMEM)
SMEM = pl.BlockSpec(memory_space=pltpu.SMEM)
ANY = pl.BlockSpec(memory_space=pl.ANY)
WIDTH = (QH + 1) * HD
SMALL = pl.CostEstimate(flops=1024, bytes_accessed=1024, transcendentals=0)


def params(megabytes):
    return pltpu.CompilerParams(vmem_limit_bytes=megabytes << 20)


def normalize(own, others, gain_own, gain_other, place, normed, to, rows):
    half = own.shape[1]
    mine = pl.multiple_of(place[0] * half, half)
    theirs = pl.multiple_of((1 - place[0]) * half, half)

    def run(other):
        @pl.loop(0, rows // 16)
        def _(step):
            at = pl.ds(pl.multiple_of(step * 16, 16), 16)
            put = pl.ds(pl.multiple_of(step * 16 + to, 16), 16)
            a = own[at, :].astype(F32)
            b = other[at, :].astype(F32)
            total = jnp.sum(a * a + b * b, axis=1, keepdims=True)
            scale = lax.rsqrt(total / (2 * half) + eps_norm)
            normed[put, pl.ds(mine, half)] = (a * scale * gain_own[...]).astype(BF)
            normed[put, pl.ds(theirs, half)] = (b * scale * gain_other[...]).astype(BF)

    for use, other in others:
        if use is None:
            run(other)
        else:
            pl.when(use)(functools.partial(run, other))


def fin_project_kernel(
    place, own, other, near_own, near_other, gain_own, gain_other, q_gain, k_gain, cos, sin, wq, wk, wv,
    out, normed, weights, sems,
):
    copies = []
    for n in range(7):
        source = wq.at[:, pl.ds(n * 256, 256)] if n < 5 else (wk if n == 5 else wv)
        copies.append(pltpu.make_async_copy(source, weights.at[n], sems.at[n]))
        copies[-1].start()
    rows = own.shape[0]
    normalize(own, [(None, other)], gain_own, gain_other, place, normed, 0, rows)
    normalize(near_own, [(None, near_other)], gain_own, gain_other, place, normed, rows, rows)
    for n in range(7):
        copies[n].wait()
        gain = q_gain if n < 5 else k_gain
        project_columns(n, normed[...], weights[n], gain, cos, sin, out, out, QH * HD)


def fin_project(shared, turn, arrays):
    place, gain_own, gain_other, q_gain, k_gain, *weights = shared
    rows = 2 * arrays[0].shape[0]
    return pl.pallas_call(
        fin_project_kernel,
        out_shape=jax.ShapeDtypeStruct((rows, (QH + 2 * KVH) * HD), BF),
        in_specs=[SMEM] + [VMEM] * 10 + [ANY] * 3,
        out_specs=VMEM,
        scratch_shapes=[
            pltpu.VMEM((rows, 5120), BF),
            pltpu.VMEM((7, 5120, 256), BF),
            pltpu.SemaphoreType.DMA((7,)),
        ],
        compiler_params=params(52),
        cost_estimate=SMALL,
    )(place, *arrays, gain_own, gain_other, q_gain, k_gain, *turn, *weights)


def kv_kernel(
    count, place, gain_own, gain_other, k_gain, own, *rest,
):
    others, (cos, sin, wk, wv, kv_out, normed, weights, sems) = rest[:count], rest[count:]
    copies = [pltpu.make_async_copy(w, weights.at[i], sems.at[i]) for i, w in enumerate((wk, wv))]

    @pl.when(pl.program_id(0) == 0)
    def _():
        for copy in copies:
            copy.start()

    uses = [(None, others[0])]
    if count == 2:
        uses = [(place[1] != 0, others[0]), (place[1] == 0, others[1])]
    normalize(own, uses, gain_own, gain_other, place, normed, 0, own.shape[0])

    @pl.when(pl.program_id(0) == 0)
    def _():
        for copy in copies:
            copy.wait()

    for i in range(2):
        project_columns(5 + i, normed[...], weights[i], k_gain, cos, sin, None, kv_out, 0)


def kv_project(shared, turn, own, others, first, rows):
    place, gain_own, gain_other, _, k_gain, _, wk, wv = shared
    half = own.shape[1]
    tile = 128
    whole = lambda array: pl.BlockSpec(array.shape, lambda i: (0, 0))
    tiles = lambda width: pl.BlockSpec((tile, width), lambda i: (i, 0))
    from_row = lambda start, width: pl.BlockSpec((tile, width), lambda i: (i + start // tile, 0))
    later = functools.partial(from_row, first)
    return pl.pallas_call(
        functools.partial(kv_kernel, len(others)),
        grid=(rows // tile,),
        out_shape=(
            jax.ShapeDtypeStruct((rows, 2 * KVH * HD), BF),
            jax.ShapeDtypeStruct((rows, 2 * half), BF),
        ),
        in_specs=[SMEM, whole(gain_own), whole(gain_other), whole(k_gain)]
        + [later(half)] + [from_row(start, half) for _, start in others] + [later(HD)] * 2 + [ANY] * 2,
        out_specs=(tiles(2 * KVH * HD), tiles(2 * half)),
        scratch_shapes=[pltpu.VMEM((2, 2 * half, 256), BF), pltpu.SemaphoreType.DMA((2,))],
        compiler_params=params(40),
        cost_estimate=SMALL,
    )(place, gain_own, gain_other, k_gain, own, *[array for array, _ in others], *turn, wk, wv)


def project_columns(n, normed, weight, gain, cos, sin, q_out, kv_out, shift):
    raw = jnp.dot(normed, weight, preferred_element_type=F32)
    for part in range(2):
        piece = raw[:, part * HD:(part + 1) * HD]
        if n == 6:
            kv_out[:, shift + (KVH + part) * HD:shift + (KVH + part + 1) * HD] = piece.astype(BF)
            continue
        mean = jnp.sum(piece * piece, axis=1, keepdims=True) * (1.0 / HD)
        piece = piece * lax.rsqrt(mean + eps_norm) * gain[...]
        turned = pltpu.roll(piece, HD // 2, 1)
        piece = (piece * cos[...] + turned * sin[...]).astype(BF)
        if n < 5:
            q_out[:, n * 256 + part * HD:n * 256 + (part + 1) * HD] = piece
        else:
            kv_out[:, shift + part * HD:shift + (part + 1) * HD] = piece


def queries_kernel(q_gain, cos, sin, wq, normed, out):
    project_columns(0, normed[...], wq[...], q_gain, cos, sin, out, None, 0)


def project_queries(shared, turn, normed, first):
    q_gain, wq = shared[3], shared[5]
    rows, depth = normed.shape
    whole = lambda array: pl.BlockSpec(array.shape, lambda i: (0, 0))
    turned = pl.BlockSpec((rows, HD), lambda i: (first // rows, 0))
    return pl.pallas_call(
        queries_kernel,
        grid=(5,),
        out_shape=jax.ShapeDtypeStruct((rows, QH * HD), BF),
        in_specs=[whole(q_gain), turned, turned, pl.BlockSpec((depth, 256), lambda i: (0, i)), whole(normed)],
        out_specs=pl.BlockSpec((rows, 256), lambda i: (0, i)),
        compiler_params=params(40),
        cost_estimate=SMALL,
    )(q_gain, *turn, wq, normed)


def guard(kv, count, keys, values):
    rows = kv.shape[0]
    live = lax.broadcasted_iota(jnp.int32, (rows, HD), 0) < count
    ones = jnp.where(live, 1.0, 0.0).astype(BF)
    for g in range(KVH):
        key = kv[:, g * HD:(g + 1) * HD].astype(F32)
        keys[:, g * HD:(g + 1) * HD] = jnp.where(live, key, key[0:1, :]).astype(BF)
        value = kv[:, (KVH + g) * HD:(KVH + g + 1) * HD].astype(F32)
        values[:, 2 * g * HD:(2 * g + 1) * HD] = jnp.where(live, value, 0.0).astype(BF)
        values[:, (2 * g + 1) * HD:(2 * g + 2) * HD] = ones


def ctx_kernel(first, info, anchor, q, kv, *refs):
    out, keys, values, own_keys, own_values = refs[-5:]
    position, own_length, anchor_length = info[0], info[1], info[2]
    guard(anchor, jnp.where(position > 0, anchor_length, 0), keys, values)
    own_keys[...] = kv[:, :KVH * HD]
    for g in range(KVH):
        own_values[:, 2 * g * HD:(2 * g + 1) * HD] = kv[:, (KVH + g) * HD:(KVH + g + 1) * HD]
        own_values[:, (2 * g + 1) * HD:(2 * g + 2) * HD] = jnp.ones((kv.shape[0], HD), BF)
    tile = 128
    row = lax.broadcasted_iota(jnp.int32, (tile, HD), 0)
    causal = lax.broadcasted_iota(jnp.int32, (tile, tile), 1) <= lax.broadcasted_iota(
        jnp.int32, (tile, tile), 0
    )
    for start in range(0, out.shape[0], tile):
        before = first + start
        at = put = slice(start, start + tile)
        live = row + before < own_length
        for h in range(QH):
            g = h // GROUP
            here, there = slice(h * HD, (h + 1) * HD), slice(g * HD, (g + 1) * HD)
            both_columns = slice(2 * g * HD, (2 * g + 2) * HD)
            query = q[at, here]
            scores = [lax.dot_general(query, keys[:, there], NT, preferred_element_type=F32)]
            if before:
                scores.append(
                    lax.dot_general(query, own_keys[:before, there], NT, preferred_element_type=F32)
                )
            last = lax.dot_general(
                query, own_keys[before:before + tile, there], NT, preferred_element_type=F32
            )
            scores.append(jnp.where(causal, last, masked_score))
            peak = functools.reduce(
                jnp.maximum, [jnp.max(score, axis=1, keepdims=True) for score in scores]
            ) * score_factor
            p = [jnp.exp2(score * score_factor - peak).astype(BF) for score in scores]
            mixed = jnp.dot(p[0], values[:, both_columns], preferred_element_type=F32)
            if before:
                mixed += jnp.dot(p[1], own_values[:before, both_columns], preferred_element_type=F32)
            mixed += jnp.dot(
                p[-1], own_values[before:before + tile, both_columns], preferred_element_type=F32
            )
            result = mixed[:, :HD] / mixed[:, HD:]
            out[put, here] = jnp.where(live, result, 0.0).astype(BF)


def ctx_attention(first, rows, info, q, anchor, kv, base):
    count = kv.shape[0]
    extra = [] if base is None else [base]
    return pl.pallas_call(
        functools.partial(ctx_kernel, first),
        grid=(1,),
        out_shape=jax.ShapeDtypeStruct((count, QH * HD), BF),
        in_specs=[SMEM] + [VMEM] * 3 + [pl.BlockSpec(memory_space=pl.ANY)] * len(extra),
        out_specs=pl.BlockSpec((rows, QH * HD), lambda i: (first // rows, 0)),
        scratch_shapes=[
            pltpu.VMEM((count, KVH * HD), BF),
            pltpu.VMEM((count, 2 * KVH * HD), BF),
            pltpu.VMEM((count, KVH * HD), BF),
            pltpu.VMEM((count, 2 * KVH * HD), BF),
        ],
        input_output_aliases={4: 0} if extra else {},
        compiler_params=params(10),
        cost_estimate=SMALL,
    )(info, anchor, q, kv, *extra)


def store_stats(out, at, peaks, totals):
    lane = lax.broadcasted_iota(jnp.int32, (at.stop - at.start, HD), 1)
    peak, total = jnp.zeros(lane.shape, F32), jnp.zeros(lane.shape, F32)
    for h in range(QH):
        peak = jnp.where(lane == h, peaks[h], peak)
        total = jnp.where(lane == h, totals[h], total)
    high = total.astype(BF).astype(F32)
    stats = peak + pltpu.roll(high, 16, 1) + pltpu.roll(total - high, 32, 1)
    out[at, QH * HD:] = stats.astype(BF)


def fin_kernel(first, count, info, q, *refs):
    kvs = refs[:count]
    out, keys, values, joined = refs[count:]
    own_length = info[1]
    to = 0
    for kv in kvs:
        joined[to:to + kv.shape[0], :] = kv[...]
        to += kv.shape[0]
    guard(joined, own_length - first, keys, values)
    floor = jnp.where(own_length > first, 0.0, masked_score)
    tile = 256
    for start in range(0, q.shape[0], tile):
        at = slice(start, start + tile)
        peaks, totals = [], []
        for h in range(QH):
            g = h // GROUP
            here, there = slice(h * HD, (h + 1) * HD), slice(g * HD, (g + 1) * HD)
            score = lax.dot_general(q[at, here], keys[:, there], NT, preferred_element_type=F32)
            peak = (jnp.max(score, axis=1, keepdims=True) * score_factor).astype(BF).astype(F32)
            p = jnp.exp2(score * score_factor - peak).astype(BF)
            mixed = jnp.dot(p, values[:, 2 * g * HD:(2 * g + 2) * HD], preferred_element_type=F32)
            out[at, here] = mixed[:, :HD].astype(BF)
            peaks.append(peak + floor)
            totals.append(mixed[:, HD:])
        store_stats(out, at, peaks, totals)


def fin_attention(first, info, q, kvs):
    rows, keys = q.shape[0], sum(kv.shape[0] for kv in kvs)
    return pl.pallas_call(
        functools.partial(fin_kernel, first, len(kvs)),
        out_shape=jax.ShapeDtypeStruct((rows, WIDTH), BF),
        in_specs=[SMEM] + [VMEM] * (1 + len(kvs)),
        out_specs=VMEM,
        scratch_shapes=[
            pltpu.VMEM((keys, KVH * HD), BF),
            pltpu.VMEM((keys, 2 * KVH * HD), BF),
            pltpu.VMEM((keys, 2 * KVH * HD), BF),
        ],
        compiler_params=params(10),
        cost_estimate=SMALL,
    )(info, q, *kvs)


def self_kernel(info, ids, q, kv, kv_across, out):
    rows = out.shape[0]
    shift = QH * HD
    queries = info[0] * rows + lax.broadcasted_iota(jnp.int32, (rows, 512), 0)
    allowed = [ids[:, :512] <= queries, ids[:, 512:] <= queries]
    peaks, totals = [], []
    for h in range(QH):
        g = h // GROUP
        here = slice(h * HD, (h + 1) * HD)
        there = slice(shift + g * HD, shift + (g + 1) * HD)
        value = slice(shift + (KVH + g) * HD, shift + (KVH + g + 1) * HD)
        scores = [
            jnp.where(
                mask, lax.dot_general(q[:rows, here], part[:, there], NT, preferred_element_type=F32), masked_score
            )
            for mask, part in zip(allowed, (kv, kv_across))
        ]
        peak = jnp.maximum(*[jnp.max(score, axis=1, keepdims=True) for score in scores])
        peak = (peak * score_factor).astype(BF).astype(F32)
        p = [jnp.exp2(score * score_factor - peak) for score in scores]
        mixed = sum(
            jnp.dot(weight.astype(BF), part[:, value], preferred_element_type=F32)
            for weight, part in zip(p, (kv, kv_across))
        )
        out[:, here] = mixed.astype(BF)
        peaks.append(peak)
        totals.append(sum(jnp.sum(weight, axis=1, keepdims=True) for weight in p))
    store_stats(out, slice(0, rows), peaks, totals)


def self_attention(info, ids, q, kv, kv_across, rows):
    return pl.pallas_call(
        self_kernel,
        out_shape=jax.ShapeDtypeStruct((rows, WIDTH), BF),
        in_specs=[SMEM] + [VMEM] * 4,
        out_specs=VMEM,
        compiler_params=params(10),
        cost_estimate=SMALL,
    )(info, ids, q, kv, kv_across)


def merge_kernel(count, final, info, *refs):
    parts, outs = refs[:count], refs[count:]
    rows = outs[0].shape[0]
    tile = min(rows, 64)
    lane = lax.broadcasted_iota(jnp.int32, (tile, HD), 1)
    for k, out in enumerate(outs):
        for start in range(0, rows, tile):
            if len(outs) == 4:
                first = pl.multiple_of(lax.rem(info[0] + k, 4) * rows, rows) + start
                at = pl.ds(pl.multiple_of(first, min(tile, 16)), tile)
            else:
                at = slice(k * rows + start, k * rows + start + tile)
            to = slice(start, start + tile)
            stats = [part[at, QH * HD:].astype(F32) for part in parts]
            top = functools.reduce(jnp.maximum, stats)
            weights = [jnp.exp2(jnp.where(lane < QH, stat - top, 0.0)) for stat in stats]
            totals = [pltpu.roll(stat, HD - 16, 1) + pltpu.roll(stat, HD - 32, 1) for stat in stats]
            total = sum(w * t for w, t in zip(weights, totals))
            if final:
                inverse = 1.0 / jnp.where(lane < QH, total, 1.0)
                weights = [w * inverse for w in weights]
            for h in range(QH):
                here = slice(h * HD, (h + 1) * HD)
                mixed = sum(
                    part[at, here].astype(F32) * w[:, h:h + 1] for part, w in zip(parts, weights)
                )
                out[to, here] = mixed.astype(BF)
            if not final:
                total = jnp.where(lane < QH, total, 0.0)
                top = jnp.where(lane < QH, top, 0.0)
                high = total.astype(BF).astype(F32)
                packed = top + pltpu.roll(high, 16, 1) + pltpu.roll(total - high, 32, 1)
                out[to, QH * HD:] = packed.astype(BF)


def merge(parts, count=1, turn=None, final=False):
    rows = parts[0].shape[0] // count
    turn = jnp.zeros((1,), jnp.int32) if turn is None else turn.reshape(1)
    shape = jax.ShapeDtypeStruct((rows, QH * HD if final else WIDTH), BF)
    return pl.pallas_call(
        functools.partial(merge_kernel, len(parts), final),
        out_shape=(shape,) * count,
        in_specs=[SMEM] + [VMEM] * len(parts),
        out_specs=(VMEM,) * count,
        compiler_params=params(10),
        cost_estimate=SMALL,
    )(turn, *parts)


def join_kernel(*refs):
    to = 0
    for ref in refs[:-1]:
        refs[-1][to:to + ref.shape[0], :] = ref[...]
        to += ref.shape[0]


def join(*arrays):
    return pl.pallas_call(
        join_kernel,
        out_shape=jax.ShapeDtypeStruct((sum(a.shape[0] for a in arrays), arrays[0].shape[1]), BF),
        in_specs=[VMEM] * len(arrays),
        out_specs=VMEM,
        compiler_params=params(10),
        cost_estimate=SMALL,
    )(*arrays)


def send_on(arrays, to):
    return [lax.ppermute(array, "seq", to(k)) for k, array in enumerate(arrays) if k]


def broadcast_stages(seq):
    l, x, z, c = coords(seq)
    return [
        (route_from(lambda l, x, z, c: (l, x, z, c) == (0, 0, 0, 0), lambda l, x, z, c: (l, x, 2, c)),
         (l == 0) & (x == 0) & (z == 2) & (c == 0)),
        (route_from(lambda l, x, z, c: l == 0 and x == 0 and z in (0, 2) and c == 0, lambda l, x, z, c: (l, x, z + 1, c)),
         (l == 0) & (x == 0) & (z % 2 == 1) & (c == 0)),
        (route_from(lambda l, x, z, c: l == 0 and x == 0 and c == 0, lambda l, x, z, c: (l, 2, z, c)),
         (l == 0) & (x == 2) & (c == 0)),
        (route_from(lambda l, x, z, c: l == 0 and x in (0, 2) and c == 0, lambda l, x, z, c: (l, x + 1, z, c)),
         (l == 0) & (x % 2 == 1) & (c == 0)),
        (route_from(lambda l, x, z, c: l == 0 and c == 0, lambda l, x, z, c: (1, x, z, c)),
         (l == 1) & (c == 0)),
        (route_from(lambda l, x, z, c: c == 0, lambda l, x, z, c: (l, x, z, 1)), c == 1),
    ]


def route_from(holds, move):
    return [(s, number(*move(*coords(s)))) for s in range(64) if holds(*coords(s))]


def turns(positions):
    exponent = jnp.arange(HD // 2, dtype=F32) * (-2.0 / HD)
    frequency = jnp.power(F32(rope_base), exponent)
    angles = positions.astype(F32)[:, None] * frequency[None, :]
    cos, sin = jnp.cos(angles), jnp.sin(angles)
    return jnp.concatenate([cos, cos], axis=1), jnp.concatenate([-sin, sin], axis=1)


def tie(*values):
    return lax.optimization_barrier(values)


def local(ctx_hidden, fin_hidden, lengths, ln_gain, q_weight, k_weight, v_weight, q_gain, k_gain):
    ctx_count, half = ctx_hidden.shape
    fin_count = fin_hidden.shape[0]
    head = lax.axis_index("head").astype(jnp.int32)
    seq = lax.axis_index("seq").astype(jnp.int32)
    axes = ("seq", "head")
    own_gain = ln_gain.reshape(1, half)
    high = lax.reduce_precision(own_gain, 8, 7)
    middle = lax.reduce_precision(own_gain - high, 8, 7)
    low = own_gain - high - middle
    pieces = [piece.astype(BF) for piece in (high, middle, low)]
    sent = jnp.concatenate([fin_hidden] + pieces + [jnp.zeros((13, half), BF)], axis=0)
    received = lax.ppermute(sent, "head", SWAP)
    near_own = lax.ppermute(fin_hidden, "seq", TO_Y)
    near_other = lax.ppermute(fin_hidden, axes, TO_CROSS)
    split = ctx_count // 2
    soon = lax.ppermute(ctx_hidden[:split], "head", SWAP)
    ahead = lax.ppermute(ctx_hidden[split:], axes, SWAP_FIRST)
    tail = split + split // 2
    others = lax.ppermute(ctx_hidden[split:tail], axes, SWAP_REST)
    last = lax.ppermute(ctx_hidden[tail:], axes, SWAP_REST)

    weights = (q_weight, k_weight, v_weight)
    block_ids = jnp.arange(64, dtype=jnp.int32)
    own_start = jnp.sum(jnp.where(block_ids < seq, lengths, 0))
    own_length = jnp.sum(jnp.where(block_ids == seq, lengths, 0))
    live_total = jnp.sum(lengths)
    my_l, my_x, my_z, my_c = coords(seq)
    near = number(1 - my_l, my_x, my_z, my_c)
    fin_ids = jnp.arange(fin_count, dtype=jnp.int32)
    fin_positions = live_total + jnp.concatenate([seq * fin_count + fin_ids, near * fin_count + fin_ids])

    info = jnp.stack([seq, own_length, lengths[0], jnp.int32(fin_count)])
    other_gain = sum(received[fin_count + i:fin_count + i + 1].astype(F32) for i in range(3))
    shared = (
        jnp.stack([head, seq]), own_gain, other_gain, q_gain.reshape(1, HD), k_gain.reshape(1, HD), *weights,
    )
    own_qkv = fin_project(shared, turns(fin_positions), (fin_hidden, received, near_own, near_other))
    own_qkv, own_start = tie(own_qkv, own_start)
    turn = turns(own_start + jnp.arange(ctx_count, dtype=jnp.int32))
    def double(array, pairs):
        return lax.ppermute(array, "seq", pairs)

    passed = double(own_qkv, to_x(1))
    own_qkv, passed, turn = tie(own_qkv, passed, turn)
    gathered = join(own_qkv, passed)
    gathered = join(gathered, double(gathered, to_x(2)))
    gathered, soon = tie(gathered, soon)
    passed = double(gathered, to_z(1))
    kv_soon, normed = kv_project(shared, turn, ctx_hidden, ((soon, 0),), 0, split)
    passed, kv_soon = tie(passed, kv_soon)
    gathered = join(gathered, passed)
    passed = double(gathered, to_z(2))
    q_soon = project_queries(shared, turn, normed, 0)
    q_soon, ahead = tie(q_soon, ahead)
    kv_ahead = kv_project(shared, turn, ctx_hidden, ((ahead, 0),), split, split)[0]
    kv_ahead, others = tie(kv_ahead, others)
    stages = broadcast_stages(seq)
    anchor = join(kv_soon, kv_ahead)

    def send(stage):
        return lax.ppermute(anchor, "seq", stages[stage][0])

    def take(stage):
        return jnp.where(stages[stage][1], arrived, anchor)

    arrived = send(0)
    kv_next, normed = kv_project(shared, turn, ctx_hidden, ((others, 0), (ahead, 0)), split, split // 2)
    passed, kv_next = tie(passed, kv_next)
    gathered = join(gathered, passed)
    across = lax.ppermute(gathered, "seq", TO_CORE)
    q_next = project_queries(shared, turn, normed, split)
    q_next, arrived, across = tie(q_next, arrived, across)
    anchor = take(0)
    arrived = send(1)
    slot = jnp.arange(64, dtype=jnp.int32)
    owner = number(my_l ^ (slot % 2), my_x ^ (slot // 2 % 4), my_z ^ (slot // 8 % 4), my_c ^ (slot // 32))
    ids = (owner[:, None] * fin_count + fin_ids[None, :]).reshape(1, -1)
    own_part = self_attention(info, ids, own_qkv, gathered, across, fin_count)
    own_part, last = tie(own_part, last)
    kv_last, normed = kv_project(shared, turn, ctx_hidden, ((last, 0), (ahead, split // 2)), tail, split // 2)
    kv_last, arrived = tie(kv_last, arrived)
    anchor = take(1)
    arrived = send(2)
    kv = join(kv_soon, kv_next, kv_last)
    away = fin_attention(0, info, across, [kv])
    passed = lax.ppermute(away, "seq", TO_CORE)
    away, arrived = tie(away, arrived)
    anchor = take(2)
    arrived = send(3)
    part = fin_attention(0, info, gathered, [kv])
    part, passed, arrived = tie(part, passed, arrived)
    partial = merge([part, passed], 4)
    passed = send_on(partial, to_z)
    partial, arrived, normed = tie(partial, arrived, normed)
    anchor = take(3)
    arrived = send(4)
    q_last = project_queries(shared, turn, normed, tail)
    q_late = join(q_next, q_last)
    q_late, arrived = tie(q_late, arrived)
    anchor = take(4)
    arrived = send(5)
    passed, anchor = tie(passed, anchor)
    partial = merge([partial[0]] + passed, 4)
    passed = send_on(partial, to_x)
    partial, arrived = tie(partial, arrived)
    anchor = take(5)
    ctx_out = ctx_attention(0, split, info, q_soon, anchor, kv, None)
    passed, ctx_out = tie(passed, ctx_out)
    partial = merge([partial[0]] + passed, 2)
    passed = lax.ppermute(partial[1], "seq", TO_Y)
    partial, ctx_out = tie(partial, ctx_out)
    ctx_out = ctx_attention(split, split, info, q_late, anchor, kv, ctx_out)
    passed, ctx_out = tie(passed, ctx_out)
    fin_out = merge([partial[0], passed, own_part], final=True)[0]
    return ctx_out, fin_out


def solution(mesh):
    return jax.shard_map(
        local,
        mesh=mesh,
        in_specs=(
            P("seq", "head"),
            P("seq", "head"),
            P(),
            P("head"),
            P(None, "head"),
            P(None, "head"),
            P(None, "head"),
            P(),
            P(),
        ),
        out_specs=(P("seq", "head"), P("seq", "head")),
        check_vma=False,
    )
```

```python
import functools

import jax
import jax.numpy as jnp
from jax import lax
from jax.experimental import pallas as pl
from jax.experimental.pallas import tpu as pltpu
from jax.sharding import PartitionSpec as P

HD = 128
GROUP = 5
KVH = 2
QH = 10
eps_norm = 1e-06
rope_base = 1000000.0
masked_score = -1e30
log2e = 1.4426950408889634
score_factor = HD ** (-0.5) * log2e
CHUNK = 128
F32 = jnp.float32
BF = jnp.bfloat16
NT = (((1,), (1,)), ((), ()))
SWAP = [(0, 1), (1, 0)]


def number(l, x, z, c):
    return ((l * 4 + x) * 4 + z) * 2 + c


def coords(s):
    return s // 32, s // 8 % 4, s // 2 % 4, s % 2


def route(move):
    return [(s, number(*move(*coords(s)))) for s in range(64)]


def to_z(k):
    return route(lambda l, x, z, c: (l, x, z ^ k, c))


def to_x(k):
    return route(lambda l, x, z, c: (l, x ^ k, z, c))


def both(move):
    pairs = []
    for s in range(64):
        l, x, z, c = coords(s)
        for h in range(2):
            to_l, to_h = move(l, h)
            pairs.append((2 * s + h, 2 * number(to_l, x, z, c) + to_h))
    return pairs


TO_CROSS = both(lambda l, h: (1 - l, 1 - h))
SWAP_FIRST = [(0, 1), (1, 0)]
SWAP_REST = [pair for pair in both(lambda l, h: (l, 1 - h)) if pair[0] > 1]
TO_Y = route(lambda l, x, z, c: (1 - l, x, z, c))
TO_CORE = route(lambda l, x, z, c: (l, x, z, 1 - c))


VMEM = pl.BlockSpec(memory_space=pltpu.VMEM)
SMEM = pl.BlockSpec(memory_space=pltpu.SMEM)
ANY = pl.BlockSpec(memory_space=pl.ANY)
WIDTH = (QH + 1) * HD


def cost(time):
    return pl.CostEstimate(
        flops=int(time * 1.15e9), bytes_accessed=int(time * 1e6), transcendentals=0
    )


def params(megabytes):
    return pltpu.CompilerParams(vmem_limit_bytes=megabytes << 20)


def normalize(own, others, gain_own, gain_other, place, normed, to, rows):
    half = own.shape[1]
    mine = pl.multiple_of(place[0] * half, half)
    theirs = pl.multiple_of((1 - place[0]) * half, half)

    def run(other):
        @pl.loop(0, rows // 16)
        def _(step):
            at = pl.ds(pl.multiple_of(step * 16, 16), 16)
            put = pl.ds(pl.multiple_of(step * 16 + to, 16), 16)
            a = own[at, :].astype(F32)
            b = other[at, :].astype(F32)
            total = jnp.sum(a * a + b * b, axis=1, keepdims=True)
            scale = lax.rsqrt(total / (2 * half) + eps_norm)
            normed[put, pl.ds(mine, half)] = (a * scale * gain_own[...]).astype(BF)
            normed[put, pl.ds(theirs, half)] = (b * scale * gain_other[...]).astype(BF)

    for use, other in others:
        if use is None:
            run(other)
        else:
            pl.when(use)(functools.partial(run, other))


def fin_project_kernel(
    place, own, other, near_own, near_other, gain_own, gain_other, q_gain, k_gain, cos, sin, wq, wk, wv,
    out, normed, weights, sems,
):
    copies = []
    for n in range(7):
        source = wq.at[:, pl.ds(n * 256, 256)] if n < 5 else (wk if n == 5 else wv)
        copies.append(pltpu.make_async_copy(source, weights.at[n], sems.at[n]))
        copies[-1].start()
    rows = own.shape[0]
    normalize(own, [(None, other)], gain_own, gain_other, place, normed, 0, rows)
    normalize(near_own, [(None, near_other)], gain_own, gain_other, place, normed, rows, rows)
    for n in range(7):
        copies[n].wait()
        gain = q_gain if n < 5 else k_gain
        project_columns(n, normed[...], weights[n], gain, cos, sin, out, out, QH * HD)


def fin_project(shared, turn, arrays):
    place, gain_own, gain_other, q_gain, k_gain, *weights = shared
    rows = 2 * arrays[0].shape[0]
    return pl.pallas_call(
        fin_project_kernel,
        out_shape=jax.ShapeDtypeStruct((rows, (QH + 2 * KVH) * HD), BF),
        in_specs=[SMEM] + [VMEM] * 10 + [ANY] * 3,
        out_specs=VMEM,
        scratch_shapes=[
            pltpu.VMEM((rows, 5120), BF),
            pltpu.VMEM((7, 5120, 256), BF),
            pltpu.SemaphoreType.DMA((7,)),
        ],
        compiler_params=params(52),
        cost_estimate=cost(0.1),
    )(place, *arrays, gain_own, gain_other, q_gain, k_gain, *turn, *weights)


def kv_kernel(
    count, place, gain_own, gain_other, k_gain, own, *rest,
):
    others, (cos, sin, wk, wv, kv_out, normed, weights, sems) = rest[:count], rest[count:]
    copies = [pltpu.make_async_copy(w, weights.at[i], sems.at[i]) for i, w in enumerate((wk, wv))]

    @pl.when(pl.program_id(0) == 0)
    def _():
        for copy in copies:
            copy.start()

    uses = [(None, others[0])]
    if count == 2:
        uses = [(place[1] != 0, others[0]), (place[1] == 0, others[1])]
    normalize(own, uses, gain_own, gain_other, place, normed, 0, own.shape[0])

    @pl.when(pl.program_id(0) == 0)
    def _():
        for copy in copies:
            copy.wait()

    for i in range(2):
        project_columns(5 + i, normed[...], weights[i], k_gain, cos, sin, None, kv_out, 0)


def kv_project(shared, turn, own, others, first, rows):
    place, gain_own, gain_other, _, k_gain, _, wk, wv = shared
    half = own.shape[1]
    tile = 128
    whole = lambda array: pl.BlockSpec(array.shape, lambda i: (0, 0))
    tiles = lambda width: pl.BlockSpec((tile, width), lambda i: (i, 0))
    from_row = lambda start, width: pl.BlockSpec((tile, width), lambda i: (i + start // tile, 0))
    later = functools.partial(from_row, first)
    return pl.pallas_call(
        functools.partial(kv_kernel, len(others)),
        grid=(rows // tile,),
        out_shape=(
            jax.ShapeDtypeStruct((rows, 2 * KVH * HD), BF),
            jax.ShapeDtypeStruct((rows, 2 * half), BF),
        ),
        in_specs=[SMEM, whole(gain_own), whole(gain_other), whole(k_gain)]
        + [later(half)] + [from_row(start, half) for _, start in others] + [later(HD)] * 2 + [ANY] * 2,
        out_specs=(tiles(2 * KVH * HD), tiles(2 * half)),
        scratch_shapes=[pltpu.VMEM((2, 2 * half, 256), BF), pltpu.SemaphoreType.DMA((2,))],
        compiler_params=params(40),
        cost_estimate=cost(0.02 * rows / 128),
    )(place, gain_own, gain_other, k_gain, own, *[array for array, _ in others], *turn, wk, wv)


def project_columns(n, normed, weight, gain, cos, sin, q_out, kv_out, shift):
    raw = jnp.dot(normed, weight, preferred_element_type=F32)
    for part in range(2):
        piece = raw[:, part * HD:(part + 1) * HD]
        if n == 6:
            kv_out[:, shift + (KVH + part) * HD:shift + (KVH + part + 1) * HD] = piece.astype(BF)
            continue
        mean = jnp.sum(piece * piece, axis=1, keepdims=True) * (1.0 / HD)
        piece = piece * lax.rsqrt(mean + eps_norm) * gain[...]
        turned = pltpu.roll(piece, HD // 2, 1)
        piece = (piece * cos[...] + turned * sin[...]).astype(BF)
        if n < 5:
            q_out[:, n * 256 + part * HD:n * 256 + (part + 1) * HD] = piece
        else:
            kv_out[:, shift + part * HD:shift + (part + 1) * HD] = piece


def queries_kernel(q_gain, cos, sin, wq, normed, out):
    project_columns(0, normed[...], wq[...], q_gain, cos, sin, out, None, 0)


def project_queries(shared, turn, normed, first, time=8):
    q_gain, wq = shared[3], shared[5]
    rows, depth = normed.shape
    whole = lambda array: pl.BlockSpec(array.shape, lambda i: (0, 0))
    turned = pl.BlockSpec((rows, HD), lambda i: (first // rows, 0))
    return pl.pallas_call(
        queries_kernel,
        grid=(5,),
        out_shape=jax.ShapeDtypeStruct((rows, QH * HD), BF),
        in_specs=[whole(q_gain), turned, turned, pl.BlockSpec((depth, 256), lambda i: (0, i)), whole(normed)],
        out_specs=pl.BlockSpec((rows, 256), lambda i: (0, i)),
        compiler_params=params(40),
        cost_estimate=cost(time),
    )(q_gain, *turn, wq, normed)


def guard(kv, count, keys, values):
    rows = kv.shape[0]
    live = lax.broadcasted_iota(jnp.int32, (rows, HD), 0) < count
    ones = jnp.where(live, 1.0, 0.0).astype(BF)
    for g in range(KVH):
        key = kv[:, g * HD:(g + 1) * HD].astype(F32)
        keys[:, g * HD:(g + 1) * HD] = jnp.where(live, key, key[0:1, :]).astype(BF)
        value = kv[:, (KVH + g) * HD:(KVH + g + 1) * HD].astype(F32)
        values[:, 2 * g * HD:(2 * g + 1) * HD] = jnp.where(live, value, 0.0).astype(BF)
        values[:, (2 * g + 1) * HD:(2 * g + 2) * HD] = ones


def ctx_kernel(first, info, anchor, q, kv, *refs):
    out, keys, values, own_keys, own_values = refs[-5:]
    position, own_length, anchor_length = info[0], info[1], info[2]
    guard(anchor, jnp.where(position > 0, anchor_length, 0), keys, values)
    own_keys[...] = kv[:, :KVH * HD]
    for g in range(KVH):
        own_values[:, 2 * g * HD:(2 * g + 1) * HD] = kv[:, (KVH + g) * HD:(KVH + g + 1) * HD]
        own_values[:, (2 * g + 1) * HD:(2 * g + 2) * HD] = jnp.ones((kv.shape[0], HD), BF)
    tile = 128
    row = lax.broadcasted_iota(jnp.int32, (tile, HD), 0)
    causal = lax.broadcasted_iota(jnp.int32, (tile, tile), 1) <= lax.broadcasted_iota(
        jnp.int32, (tile, tile), 0
    )
    for start in range(0, out.shape[0], tile):
        before = first + start
        at = put = slice(start, start + tile)
        live = row + before < own_length
        for h in range(QH):
            g = h // GROUP
            here, there = slice(h * HD, (h + 1) * HD), slice(g * HD, (g + 1) * HD)
            both_columns = slice(2 * g * HD, (2 * g + 2) * HD)
            query = q[at, here]
            scores = [lax.dot_general(query, keys[:, there], NT, preferred_element_type=F32)]
            if before:
                scores.append(
                    lax.dot_general(query, own_keys[:before, there], NT, preferred_element_type=F32)
                )
            last = lax.dot_general(
                query, own_keys[before:before + tile, there], NT, preferred_element_type=F32
            )
            scores.append(jnp.where(causal, last, masked_score))
            peak = functools.reduce(
                jnp.maximum, [jnp.max(score, axis=1, keepdims=True) for score in scores]
            ) * score_factor
            p = [jnp.exp2(score * score_factor - peak).astype(BF) for score in scores]
            mixed = jnp.dot(p[0], values[:, both_columns], preferred_element_type=F32)
            if before:
                mixed += jnp.dot(p[1], own_values[:before, both_columns], preferred_element_type=F32)
            mixed += jnp.dot(
                p[-1], own_values[before:before + tile, both_columns], preferred_element_type=F32
            )
            result = mixed[:, :HD] / mixed[:, HD:]
            out[put, here] = jnp.where(live, result, 0.0).astype(BF)


def ctx_attention(first, rows, info, q, anchor, kv, base):
    count = kv.shape[0]
    extra = [] if base is None else [base]
    return pl.pallas_call(
        functools.partial(ctx_kernel, first),
        grid=(1,),
        out_shape=jax.ShapeDtypeStruct((count, QH * HD), BF),
        in_specs=[SMEM] + [VMEM] * 3 + [pl.BlockSpec(memory_space=pl.ANY)] * len(extra),
        out_specs=pl.BlockSpec((rows, QH * HD), lambda i: (first // rows, 0)),
        scratch_shapes=[
            pltpu.VMEM((count, KVH * HD), BF),
            pltpu.VMEM((count, 2 * KVH * HD), BF),
            pltpu.VMEM((count, KVH * HD), BF),
            pltpu.VMEM((count, 2 * KVH * HD), BF),
        ],
        input_output_aliases={4: 0} if extra else {},
        compiler_params=params(10),
        cost_estimate=cost(5),
    )(info, anchor, q, kv, *extra)


def store_stats(out, at, peaks, totals):
    lane = lax.broadcasted_iota(jnp.int32, (at.stop - at.start, HD), 1)
    peak, total = jnp.zeros(lane.shape, F32), jnp.zeros(lane.shape, F32)
    for h in range(QH):
        peak = jnp.where(lane == h, peaks[h], peak)
        total = jnp.where(lane == h, totals[h], total)
    high = total.astype(BF).astype(F32)
    stats = peak + pltpu.roll(high, 16, 1) + pltpu.roll(total - high, 32, 1)
    out[at, QH * HD:] = stats.astype(BF)


def fin_kernel(first, count, info, q, *refs):
    kvs = refs[:count]
    out, keys, values, joined = refs[count:]
    own_length = info[1]
    to = 0
    for kv in kvs:
        joined[to:to + kv.shape[0], :] = kv[...]
        to += kv.shape[0]
    guard(joined, own_length - first, keys, values)
    floor = jnp.where(own_length > first, 0.0, masked_score)
    tile = 256
    for start in range(0, q.shape[0], tile):
        at = slice(start, start + tile)
        peaks, totals = [], []
        for h in range(QH):
            g = h // GROUP
            here, there = slice(h * HD, (h + 1) * HD), slice(g * HD, (g + 1) * HD)
            score = lax.dot_general(q[at, here], keys[:, there], NT, preferred_element_type=F32)
            peak = (jnp.max(score, axis=1, keepdims=True) * score_factor).astype(BF).astype(F32)
            p = jnp.exp2(score * score_factor - peak).astype(BF)
            mixed = jnp.dot(p, values[:, 2 * g * HD:(2 * g + 2) * HD], preferred_element_type=F32)
            out[at, here] = mixed[:, :HD].astype(BF)
            peaks.append(peak + floor)
            totals.append(mixed[:, HD:])
        store_stats(out, at, peaks, totals)


def fin_attention(first, info, q, kvs):
    rows, keys = q.shape[0], sum(kv.shape[0] for kv in kvs)
    return pl.pallas_call(
        functools.partial(fin_kernel, first, len(kvs)),
        out_shape=jax.ShapeDtypeStruct((rows, WIDTH), BF),
        in_specs=[SMEM] + [VMEM] * (1 + len(kvs)),
        out_specs=VMEM,
        scratch_shapes=[
            pltpu.VMEM((keys, KVH * HD), BF),
            pltpu.VMEM((keys, 2 * KVH * HD), BF),
            pltpu.VMEM((keys, 2 * KVH * HD), BF),
        ],
        compiler_params=params(10),
        cost_estimate=cost(5),
    )(info, q, *kvs)


def self_kernel(info, ids, q, kv, kv_across, out):
    rows = out.shape[0]
    shift = QH * HD
    queries = info[0] * rows + lax.broadcasted_iota(jnp.int32, (rows, 512), 0)
    allowed = [ids[:, :512] <= queries, ids[:, 512:] <= queries]
    peaks, totals = [], []
    for h in range(QH):
        g = h // GROUP
        here = slice(h * HD, (h + 1) * HD)
        there = slice(shift + g * HD, shift + (g + 1) * HD)
        value = slice(shift + (KVH + g) * HD, shift + (KVH + g + 1) * HD)
        scores = [
            jnp.where(
                mask, lax.dot_general(q[:rows, here], part[:, there], NT, preferred_element_type=F32), masked_score
            )
            for mask, part in zip(allowed, (kv, kv_across))
        ]
        peak = jnp.maximum(*[jnp.max(score, axis=1, keepdims=True) for score in scores])
        peak = (peak * score_factor).astype(BF).astype(F32)
        p = [jnp.exp2(score * score_factor - peak) for score in scores]
        mixed = sum(
            jnp.dot(weight.astype(BF), part[:, value], preferred_element_type=F32)
            for weight, part in zip(p, (kv, kv_across))
        )
        out[:, here] = mixed.astype(BF)
        peaks.append(peak)
        totals.append(sum(jnp.sum(weight, axis=1, keepdims=True) for weight in p))
    store_stats(out, slice(0, rows), peaks, totals)


def self_attention(info, ids, q, kv, kv_across, rows):
    return pl.pallas_call(
        self_kernel,
        out_shape=jax.ShapeDtypeStruct((rows, WIDTH), BF),
        in_specs=[SMEM] + [VMEM] * 4,
        out_specs=VMEM,
        compiler_params=params(10),
        cost_estimate=cost(5),
    )(info, ids, q, kv, kv_across)


def merge_kernel(count, final, info, *refs):
    parts, outs = refs[:count], refs[count:]
    rows = outs[0].shape[0]
    tile = min(rows, 64)
    lane = lax.broadcasted_iota(jnp.int32, (tile, HD), 1)
    for k, out in enumerate(outs):
        for start in range(0, rows, tile):
            if len(outs) == 4:
                first = pl.multiple_of(lax.rem(info[0] + k, 4) * rows, rows) + start
                at = pl.ds(pl.multiple_of(first, min(tile, 16)), tile)
            else:
                at = slice(k * rows + start, k * rows + start + tile)
            to = slice(start, start + tile)
            stats = [part[at, QH * HD:].astype(F32) for part in parts]
            top = functools.reduce(jnp.maximum, stats)
            weights = [jnp.exp2(jnp.where(lane < QH, stat - top, 0.0)) for stat in stats]
            totals = [pltpu.roll(stat, HD - 16, 1) + pltpu.roll(stat, HD - 32, 1) for stat in stats]
            total = sum(w * t for w, t in zip(weights, totals))
            if final:
                inverse = 1.0 / jnp.where(lane < QH, total, 1.0)
                weights = [w * inverse for w in weights]
            for h in range(QH):
                here = slice(h * HD, (h + 1) * HD)
                mixed = sum(
                    part[at, here].astype(F32) * w[:, h:h + 1] for part, w in zip(parts, weights)
                )
                out[to, here] = mixed.astype(BF)
            if not final:
                total = jnp.where(lane < QH, total, 0.0)
                top = jnp.where(lane < QH, top, 0.0)
                high = total.astype(BF).astype(F32)
                packed = top + pltpu.roll(high, 16, 1) + pltpu.roll(total - high, 32, 1)
                out[to, QH * HD:] = packed.astype(BF)


def merge(parts, count=1, turn=None, final=False):
    rows = parts[0].shape[0] // count
    turn = jnp.zeros((1,), jnp.int32) if turn is None else turn.reshape(1)
    shape = jax.ShapeDtypeStruct((rows, QH * HD if final else WIDTH), BF)
    return pl.pallas_call(
        functools.partial(merge_kernel, len(parts), final),
        out_shape=(shape,) * count,
        in_specs=[SMEM] + [VMEM] * len(parts),
        out_specs=(VMEM,) * count,
        compiler_params=params(10),
        cost_estimate=cost(0.3 * sum(part.shape[0] for part in parts) / 128),
    )(turn, *parts)


def join_kernel(*refs):
    to = 0
    for ref in refs[:-1]:
        refs[-1][to:to + ref.shape[0], :] = ref[...]
        to += ref.shape[0]


def join(*arrays):
    return pl.pallas_call(
        join_kernel,
        out_shape=jax.ShapeDtypeStruct((sum(a.shape[0] for a in arrays), arrays[0].shape[1]), BF),
        in_specs=[VMEM] * len(arrays),
        out_specs=VMEM,
        compiler_params=params(10),
        cost_estimate=cost(0.02),
    )(*arrays)


def send_on(arrays, to):
    return [lax.ppermute(array, "seq", to(k)) for k, array in enumerate(arrays) if k]


def broadcast_stages(seq):
    l, x, z, c = coords(seq)
    return [
        (route_from(lambda l, x, z, c: (l, x, z, c) == (0, 0, 0, 0), lambda l, x, z, c: (l, x, 2, c)),
         (l == 0) & (x == 0) & (z == 2) & (c == 0)),
        (route_from(lambda l, x, z, c: l == 0 and x == 0 and z in (0, 2) and c == 0, lambda l, x, z, c: (l, x, z + 1, c)),
         (l == 0) & (x == 0) & (z % 2 == 1) & (c == 0)),
        (route_from(lambda l, x, z, c: l == 0 and x == 0 and c == 0, lambda l, x, z, c: (l, 2, z, c)),
         (l == 0) & (x == 2) & (c == 0)),
        (route_from(lambda l, x, z, c: l == 0 and x in (0, 2) and c == 0, lambda l, x, z, c: (l, x + 1, z, c)),
         (l == 0) & (x % 2 == 1) & (c == 0)),
        (route_from(lambda l, x, z, c: l == 0 and c == 0, lambda l, x, z, c: (1, x, z, c)),
         (l == 1) & (c == 0)),
        (route_from(lambda l, x, z, c: c == 0, lambda l, x, z, c: (l, x, z, 1)), c == 1),
    ]


def route_from(holds, move):
    return [(s, number(*move(*coords(s)))) for s in range(64) if holds(*coords(s))]


def turns(positions):
    exponent = jnp.arange(HD // 2, dtype=F32) * (-2.0 / HD)
    frequency = jnp.power(F32(rope_base), exponent)
    angles = positions.astype(F32)[:, None] * frequency[None, :]
    cos, sin = jnp.cos(angles), jnp.sin(angles)
    return jnp.concatenate([cos, cos], axis=1), jnp.concatenate([-sin, sin], axis=1)


def tie(*values):
    return lax.optimization_barrier(values)


def local(ctx_hidden, fin_hidden, lengths, ln_gain, q_weight, k_weight, v_weight, q_gain, k_gain):
    ctx_count, half = ctx_hidden.shape
    fin_count = fin_hidden.shape[0]
    head = lax.axis_index("head").astype(jnp.int32)
    seq = lax.axis_index("seq").astype(jnp.int32)
    axes = ("seq", "head")
    own_gain = ln_gain.reshape(1, half)
    high = lax.reduce_precision(own_gain, 8, 7)
    middle = lax.reduce_precision(own_gain - high, 8, 7)
    low = own_gain - high - middle
    pieces = [piece.astype(BF) for piece in (high, middle, low)]
    sent = jnp.concatenate([fin_hidden] + pieces + [jnp.zeros((13, half), BF)], axis=0)
    received = lax.ppermute(sent, "head", SWAP)
    near_own = lax.ppermute(fin_hidden, "seq", TO_Y)
    near_other = lax.ppermute(fin_hidden, axes, TO_CROSS)
    split = ctx_count // 2
    soon = lax.ppermute(ctx_hidden[:split], "head", SWAP)
    ahead = lax.ppermute(ctx_hidden[split:], axes, SWAP_FIRST)
    others = lax.ppermute(ctx_hidden[split:], axes, SWAP_REST)

    weights = (q_weight, k_weight, v_weight)
    block_ids = jnp.arange(64, dtype=jnp.int32)
    own_start = jnp.sum(jnp.where(block_ids < seq, lengths, 0))
    own_length = jnp.sum(jnp.where(block_ids == seq, lengths, 0))
    live_total = jnp.sum(lengths)
    my_l, my_x, my_z, my_c = coords(seq)
    near = number(1 - my_l, my_x, my_z, my_c)
    fin_ids = jnp.arange(fin_count, dtype=jnp.int32)
    fin_positions = live_total + jnp.concatenate([seq * fin_count + fin_ids, near * fin_count + fin_ids])

    info = jnp.stack([seq, own_length, lengths[0], jnp.int32(fin_count)])
    other_gain = sum(received[fin_count + i:fin_count + i + 1].astype(F32) for i in range(3))
    shared = (
        jnp.stack([head, seq]), own_gain, other_gain, q_gain.reshape(1, HD), k_gain.reshape(1, HD), *weights,
    )
    own_qkv = fin_project(shared, turns(fin_positions), (fin_hidden, received, near_own, near_other))
    own_qkv, own_start = tie(own_qkv, own_start)
    turn = turns(own_start + jnp.arange(ctx_count, dtype=jnp.int32))
    def double(array, pairs):
        return lax.ppermute(array, "seq", pairs)

    passed = double(own_qkv, to_x(1))
    own_qkv, passed, turn = tie(own_qkv, passed, turn)
    gathered = join(own_qkv, passed)
    gathered = join(gathered, double(gathered, to_x(2)))
    passed = double(gathered, to_z(1))
    gathered, soon = tie(gathered, soon)
    kv_soon, normed = kv_project(shared, turn, ctx_hidden, ((soon, 0),), 0, split)
    passed, kv_soon = tie(passed, kv_soon)
    gathered = join(gathered, passed)
    passed = double(gathered, to_z(2))
    q_soon = project_queries(shared, turn, normed, 0, 0.1)
    q_soon, ahead = tie(q_soon, ahead)
    kv_ahead = kv_project(shared, turn, ctx_hidden, ((ahead, 0),), split, split)[0]
    stages = broadcast_stages(seq)
    anchor = join(kv_soon, kv_ahead)

    def send(stage):
        return lax.ppermute(anchor, "seq", stages[stage][0])

    def take(stage):
        return jnp.where(stages[stage][1], arrived, anchor)

    anchor, others, passed = tie(anchor, others, passed)
    arrived = send(0)
    gathered = join(gathered, passed)
    across = lax.ppermute(gathered, "seq", TO_CORE)
    kv_late, normed = kv_project(shared, turn, ctx_hidden, ((others, 0), (ahead, 0)), split, split)
    kv_late, arrived, across = tie(kv_late, arrived, across)
    anchor = take(0)
    arrived = send(1)
    kv = join(kv_soon, kv_late)
    away = fin_attention(0, info, across, [kv])
    passed = lax.ppermute(away, "seq", TO_CORE)
    away, arrived = tie(away, arrived)
    anchor = take(1)
    arrived = send(2)
    part = fin_attention(0, info, gathered, [kv])
    part, passed, normed = tie(part, passed, normed)
    partial = merge([part, passed], 4)
    passed = send_on(partial, to_z)
    partial, normed, arrived = tie(partial, normed, arrived)
    anchor = take(2)
    arrived = send(3)
    q_late = project_queries(shared, turn, normed, split)
    q_late, arrived = tie(q_late, arrived)
    anchor = take(3)
    arrived = send(4)
    slot = jnp.arange(64, dtype=jnp.int32)
    owner = number(my_l ^ (slot % 2), my_x ^ (slot // 2 % 4), my_z ^ (slot // 8 % 4), my_c ^ (slot // 32))
    ids = (owner[:, None] * fin_count + fin_ids[None, :]).reshape(1, -1)
    own_part = self_attention(info, ids, own_qkv, gathered, across, fin_count)
    passed, own_part, arrived = tie(passed, own_part, arrived)
    anchor = take(4)
    partial = merge([partial[0]] + passed, 4)
    arrived = send(5)
    passed = send_on(partial, to_x)
    partial, arrived = tie(partial, arrived)
    anchor = take(5)
    ctx_out = ctx_attention(0, split, info, q_soon, anchor, kv, None)
    passed, ctx_out = tie(passed, ctx_out)
    partial = merge([partial[0]] + passed, 2)
    passed = lax.ppermute(partial[1], "seq", TO_Y)
    partial, ctx_out = tie(partial, ctx_out)
    ctx_out = ctx_attention(split, split, info, q_late, anchor, kv, ctx_out)
    passed, ctx_out = tie(passed, ctx_out)
    fin_out = merge([partial[0], passed, own_part], final=True)[0]
    return ctx_out, fin_out


def solution(mesh):
    return jax.shard_map(
        local,
        mesh=mesh,
        in_specs=(
            P("seq", "head"),
            P("seq", "head"),
            P(),
            P("head"),
            P(None, "head"),
            P(None, "head"),
            P(None, "head"),
            P(),
            P(),
        ),
        out_specs=(P("seq", "head"), P("seq", "head")),
        check_vma=False,
    )
```

```python
import functools

import jax
import jax.numpy as jnp
from jax import lax
from jax.experimental import pallas as pl
from jax.experimental.pallas import tpu as pltpu
from jax.sharding import PartitionSpec as P

HD = 128
GROUP = 5
KVH = 2
QH = 10
eps_norm = 1e-06
rope_base = 1000000.0
masked_score = -1e30
log2e = 1.4426950408889634
score_factor = HD ** (-0.5) * log2e
CHUNK = 128
F32 = jnp.float32
BF = jnp.bfloat16
NT = (((1,), (1,)), ((), ()))
SWAP = [(0, 1), (1, 0)]


def number(l, x, z, c):
    return ((l * 4 + x) * 4 + z) * 2 + c


def coords(s):
    return s // 32, s // 8 % 4, s // 2 % 4, s % 2


def route(move):
    return [(s, number(*move(*coords(s)))) for s in range(64)]


def to_z(k):
    return route(lambda l, x, z, c: (l, x, z ^ k, c))


def to_x(k):
    return route(lambda l, x, z, c: (l, x ^ k, z, c))


def both(move):
    pairs = []
    for s in range(64):
        l, x, z, c = coords(s)
        for h in range(2):
            to_l, to_h = move(l, h)
            pairs.append((2 * s + h, 2 * number(to_l, x, z, c) + to_h))
    return pairs


TO_CROSS = both(lambda l, h: (1 - l, 1 - h))
SWAP_FIRST = [(0, 1), (1, 0)]
SWAP_REST = [pair for pair in both(lambda l, h: (l, 1 - h)) if pair[0] > 1]
TO_Y = route(lambda l, x, z, c: (1 - l, x, z, c))
TO_CORE = route(lambda l, x, z, c: (l, x, z, 1 - c))


VMEM = pl.BlockSpec(memory_space=pltpu.VMEM)
SMEM = pl.BlockSpec(memory_space=pltpu.SMEM)
ANY = pl.BlockSpec(memory_space=pl.ANY)
WIDTH = (QH + 1) * HD


def cost(time):
    return pl.CostEstimate(
        flops=int(time * 1.15e9), bytes_accessed=int(time * 1e6), transcendentals=0
    )


def params(megabytes):
    return pltpu.CompilerParams(vmem_limit_bytes=megabytes << 20)


def normalize(own, others, gain_own, gain_other, place, normed, to, rows):
    half = own.shape[1]
    mine = pl.multiple_of(place[0] * half, half)
    theirs = pl.multiple_of((1 - place[0]) * half, half)

    def run(other):
        @pl.loop(0, rows // 16)
        def _(step):
            at = pl.ds(pl.multiple_of(step * 16, 16), 16)
            put = pl.ds(pl.multiple_of(step * 16 + to, 16), 16)
            a = own[at, :].astype(F32)
            b = other[at, :].astype(F32)
            total = jnp.sum(a * a + b * b, axis=1, keepdims=True)
            scale = lax.rsqrt(total / (2 * half) + eps_norm)
            normed[put, pl.ds(mine, half)] = (a * scale * gain_own[...]).astype(BF)
            normed[put, pl.ds(theirs, half)] = (b * scale * gain_other[...]).astype(BF)

    for use, other in others:
        if use is None:
            run(other)
        else:
            pl.when(use)(functools.partial(run, other))


def fin_project_kernel(
    place, own, other, near_own, near_other, gain_own, gain_other, q_gain, k_gain, cos, sin, wq, wk, wv,
    out, normed, weights, sems,
):
    copies = []
    for n in range(7):
        source = wq.at[:, pl.ds(n * 256, 256)] if n < 5 else (wk if n == 5 else wv)
        copies.append(pltpu.make_async_copy(source, weights.at[n], sems.at[n]))
        copies[-1].start()
    rows = own.shape[0]
    normalize(own, [(None, other)], gain_own, gain_other, place, normed, 0, rows)
    normalize(near_own, [(None, near_other)], gain_own, gain_other, place, normed, rows, rows)
    for n in range(7):
        copies[n].wait()
        gain = q_gain if n < 5 else k_gain
        project_columns(n, normed[...], weights[n], gain, cos, sin, out, out, QH * HD)


def fin_project(shared, turn, arrays):
    place, gain_own, gain_other, q_gain, k_gain, *weights = shared
    rows = 2 * arrays[0].shape[0]
    return pl.pallas_call(
        fin_project_kernel,
        out_shape=jax.ShapeDtypeStruct((rows, (QH + 2 * KVH) * HD), BF),
        in_specs=[SMEM] + [VMEM] * 10 + [ANY] * 3,
        out_specs=VMEM,
        scratch_shapes=[
            pltpu.VMEM((rows, 5120), BF),
            pltpu.VMEM((7, 5120, 256), BF),
            pltpu.SemaphoreType.DMA((7,)),
        ],
        compiler_params=params(52),
        cost_estimate=cost(0.1),
    )(place, *arrays, gain_own, gain_other, q_gain, k_gain, *turn, *weights)


def kv_kernel(
    count, place, gain_own, gain_other, k_gain, own, *rest,
):
    others, (cos, sin, wk, wv, kv_out, normed, weights, sems) = rest[:count], rest[count:]
    copies = [pltpu.make_async_copy(w, weights.at[i], sems.at[i]) for i, w in enumerate((wk, wv))]

    @pl.when(pl.program_id(0) == 0)
    def _():
        for copy in copies:
            copy.start()

    uses = [(None, others[0])]
    if count == 2:
        uses = [(place[1] != 0, others[0]), (place[1] == 0, others[1])]
    normalize(own, uses, gain_own, gain_other, place, normed, 0, own.shape[0])

    @pl.when(pl.program_id(0) == 0)
    def _():
        for copy in copies:
            copy.wait()

    for i in range(2):
        project_columns(5 + i, normed[...], weights[i], k_gain, cos, sin, None, kv_out, 0)


def kv_project(shared, turn, own, others, first, rows, room=40):
    place, gain_own, gain_other, _, k_gain, _, wk, wv = shared
    half = own.shape[1]
    tile = 128
    whole = lambda array: pl.BlockSpec(array.shape, lambda i: (0, 0))
    tiles = lambda width: pl.BlockSpec((tile, width), lambda i: (i, 0))
    from_row = lambda start, width: pl.BlockSpec((tile, width), lambda i: (i + start // tile, 0))
    later = functools.partial(from_row, first)
    return pl.pallas_call(
        functools.partial(kv_kernel, len(others)),
        grid=(rows // tile,),
        out_shape=(
            jax.ShapeDtypeStruct((rows, 2 * KVH * HD), BF),
            jax.ShapeDtypeStruct((rows, 2 * half), BF),
        ),
        in_specs=[SMEM, whole(gain_own), whole(gain_other), whole(k_gain)]
        + [later(half)] + [from_row(start, half) for _, start in others] + [later(HD)] * 2 + [ANY] * 2,
        out_specs=(tiles(2 * KVH * HD), tiles(2 * half)),
        scratch_shapes=[pltpu.VMEM((2, 2 * half, 256), BF), pltpu.SemaphoreType.DMA((2,))],
        compiler_params=params(room),
        cost_estimate=cost(0.02 * rows / 128),
    )(place, gain_own, gain_other, k_gain, own, *[array for array, _ in others], *turn, wk, wv)


def project_columns(n, normed, weight, gain, cos, sin, q_out, kv_out, shift):
    raw = jnp.dot(normed, weight, preferred_element_type=F32)
    for part in range(2):
        piece = raw[:, part * HD:(part + 1) * HD]
        if n == 6:
            kv_out[:, shift + (KVH + part) * HD:shift + (KVH + part + 1) * HD] = piece.astype(BF)
            continue
        mean = jnp.sum(piece * piece, axis=1, keepdims=True) * (1.0 / HD)
        piece = piece * lax.rsqrt(mean + eps_norm) * gain[...]
        turned = pltpu.roll(piece, HD // 2, 1)
        piece = (piece * cos[...] + turned * sin[...]).astype(BF)
        if n < 5:
            q_out[:, n * 256 + part * HD:n * 256 + (part + 1) * HD] = piece
        else:
            kv_out[:, shift + part * HD:shift + (part + 1) * HD] = piece


def queries_kernel(q_gain, cos, sin, wq, normed, out):
    project_columns(0, normed[...], wq[...], q_gain, cos, sin, out, None, 0)


def project_queries(shared, turn, normed, first, time=8):
    q_gain, wq = shared[3], shared[5]
    rows, depth = normed.shape
    whole = lambda array: pl.BlockSpec(array.shape, lambda i: (0, 0))
    turned = pl.BlockSpec((rows, HD), lambda i: (first // rows, 0))
    return pl.pallas_call(
        queries_kernel,
        grid=(5,),
        out_shape=jax.ShapeDtypeStruct((rows, QH * HD), BF),
        in_specs=[whole(q_gain), turned, turned, pl.BlockSpec((depth, 256), lambda i: (0, i)), whole(normed)],
        out_specs=pl.BlockSpec((rows, 256), lambda i: (0, i)),
        compiler_params=params(40),
        cost_estimate=cost(time),
    )(q_gain, *turn, wq, normed)


def guard(kv, count, keys, values):
    rows = kv.shape[0]
    live = lax.broadcasted_iota(jnp.int32, (rows, HD), 0) < count
    ones = jnp.where(live, 1.0, 0.0).astype(BF)
    for g in range(KVH):
        key = kv[:, g * HD:(g + 1) * HD].astype(F32)
        keys[:, g * HD:(g + 1) * HD] = jnp.where(live, key, key[0:1, :]).astype(BF)
        value = kv[:, (KVH + g) * HD:(KVH + g + 1) * HD].astype(F32)
        values[:, 2 * g * HD:(2 * g + 1) * HD] = jnp.where(live, value, 0.0).astype(BF)
        values[:, (2 * g + 1) * HD:(2 * g + 2) * HD] = ones


def ctx_kernel(first, info, anchor, q, kv, *refs):
    out, keys, values, own_keys, own_values = refs[-5:]
    position, own_length, anchor_length = info[0], info[1], info[2]
    guard(anchor, jnp.where(position > 0, anchor_length, 0), keys, values)
    own_keys[...] = kv[:, :KVH * HD]
    for g in range(KVH):
        own_values[:, 2 * g * HD:(2 * g + 1) * HD] = kv[:, (KVH + g) * HD:(KVH + g + 1) * HD]
        own_values[:, (2 * g + 1) * HD:(2 * g + 2) * HD] = jnp.ones((kv.shape[0], HD), BF)
    tile = 128
    row = lax.broadcasted_iota(jnp.int32, (tile, HD), 0)
    causal = lax.broadcasted_iota(jnp.int32, (tile, tile), 1) <= lax.broadcasted_iota(
        jnp.int32, (tile, tile), 0
    )
    for start in range(0, out.shape[0], tile):
        before = first + start
        at = put = slice(start, start + tile)
        live = row + before < own_length
        for h in range(QH):
            g = h // GROUP
            here, there = slice(h * HD, (h + 1) * HD), slice(g * HD, (g + 1) * HD)
            both_columns = slice(2 * g * HD, (2 * g + 2) * HD)
            query = q[at, here]
            scores = [lax.dot_general(query, keys[:, there], NT, preferred_element_type=F32)]
            if before:
                scores.append(
                    lax.dot_general(query, own_keys[:before, there], NT, preferred_element_type=F32)
                )
            last = lax.dot_general(
                query, own_keys[before:before + tile, there], NT, preferred_element_type=F32
            )
            scores.append(jnp.where(causal, last, masked_score))
            peak = functools.reduce(
                jnp.maximum, [jnp.max(score, axis=1, keepdims=True) for score in scores]
            ) * score_factor
            p = [jnp.exp2(score * score_factor - peak).astype(BF) for score in scores]
            mixed = jnp.dot(p[0], values[:, both_columns], preferred_element_type=F32)
            if before:
                mixed += jnp.dot(p[1], own_values[:before, both_columns], preferred_element_type=F32)
            mixed += jnp.dot(
                p[-1], own_values[before:before + tile, both_columns], preferred_element_type=F32
            )
            result = mixed[:, :HD] / mixed[:, HD:]
            out[put, here] = jnp.where(live, result, 0.0).astype(BF)


def ctx_attention(first, rows, info, q, anchor, kv, base):
    count = kv.shape[0]
    extra = [] if base is None else [base]
    return pl.pallas_call(
        functools.partial(ctx_kernel, first),
        grid=(1,),
        out_shape=jax.ShapeDtypeStruct((count, QH * HD), BF),
        in_specs=[SMEM] + [VMEM] * 3 + [pl.BlockSpec(memory_space=pl.ANY)] * len(extra),
        out_specs=pl.BlockSpec((rows, QH * HD), lambda i: (first // rows, 0)),
        scratch_shapes=[
            pltpu.VMEM((count, KVH * HD), BF),
            pltpu.VMEM((count, 2 * KVH * HD), BF),
            pltpu.VMEM((count, KVH * HD), BF),
            pltpu.VMEM((count, 2 * KVH * HD), BF),
        ],
        input_output_aliases={4: 0} if extra else {},
        compiler_params=params(10),
        cost_estimate=cost(5),
    )(info, anchor, q, kv, *extra)


def store_stats(out, at, peaks, totals):
    lane = lax.broadcasted_iota(jnp.int32, (at.stop - at.start, HD), 1)
    peak, total = jnp.zeros(lane.shape, F32), jnp.zeros(lane.shape, F32)
    for h in range(QH):
        peak = jnp.where(lane == h, peaks[h], peak)
        total = jnp.where(lane == h, totals[h], total)
    high = total.astype(BF).astype(F32)
    stats = peak + pltpu.roll(high, 16, 1) + pltpu.roll(total - high, 32, 1)
    out[at, QH * HD:] = stats.astype(BF)


def fin_kernel(first, count, info, q, *refs):
    kvs = refs[:count]
    out, keys, values, joined = refs[count:]
    own_length = info[1]
    to = 0
    for kv in kvs:
        joined[to:to + kv.shape[0], :] = kv[...]
        to += kv.shape[0]
    guard(joined, own_length - first, keys, values)
    floor = jnp.where(own_length > first, 0.0, masked_score)
    tile = 256
    for start in range(0, q.shape[0], tile):
        at = slice(start, start + tile)
        peaks, totals = [], []
        for h in range(QH):
            g = h // GROUP
            here, there = slice(h * HD, (h + 1) * HD), slice(g * HD, (g + 1) * HD)
            score = lax.dot_general(q[at, here], keys[:, there], NT, preferred_element_type=F32)
            peak = (jnp.max(score, axis=1, keepdims=True) * score_factor).astype(BF).astype(F32)
            p = jnp.exp2(score * score_factor - peak).astype(BF)
            mixed = jnp.dot(p, values[:, 2 * g * HD:(2 * g + 2) * HD], preferred_element_type=F32)
            out[at, here] = mixed[:, :HD].astype(BF)
            peaks.append(peak + floor)
            totals.append(mixed[:, HD:])
        store_stats(out, at, peaks, totals)


def fin_attention(first, info, q, kvs):
    rows, keys = q.shape[0], sum(kv.shape[0] for kv in kvs)
    return pl.pallas_call(
        functools.partial(fin_kernel, first, len(kvs)),
        out_shape=jax.ShapeDtypeStruct((rows, WIDTH), BF),
        in_specs=[SMEM] + [VMEM] * (1 + len(kvs)),
        out_specs=VMEM,
        scratch_shapes=[
            pltpu.VMEM((keys, KVH * HD), BF),
            pltpu.VMEM((keys, 2 * KVH * HD), BF),
            pltpu.VMEM((keys, 2 * KVH * HD), BF),
        ],
        compiler_params=params(10),
        cost_estimate=cost(5),
    )(info, q, *kvs)


def self_kernel(info, ids, q, kv, kv_across, out):
    rows = out.shape[0]
    shift = QH * HD
    tall = GROUP * rows
    queries = info[0] * rows + lax.rem(lax.broadcasted_iota(jnp.int32, (tall, 512), 0), rows)
    allowed = [ids[:, :512] <= queries, ids[:, 512:] <= queries]
    peaks, totals = [], []
    for g in range(KVH):
        heads = range(g * GROUP, (g + 1) * GROUP)
        query = jnp.concatenate([q[:rows, h * HD:(h + 1) * HD] for h in heads], axis=0)
        there = slice(shift + g * HD, shift + (g + 1) * HD)
        value = slice(shift + (KVH + g) * HD, shift + (KVH + g + 1) * HD)
        scores = [
            jnp.where(
                mask, lax.dot_general(query, part[:, there], NT, preferred_element_type=F32), masked_score
            )
            for mask, part in zip(allowed, (kv, kv_across))
        ]
        peak = jnp.maximum(*[jnp.max(score, axis=1, keepdims=True) for score in scores])
        peak = (peak * score_factor).astype(BF).astype(F32)
        p = [jnp.exp2(score * score_factor - peak) for score in scores]
        mixed = sum(
            jnp.dot(weight.astype(BF), part[:, value], preferred_element_type=F32)
            for weight, part in zip(p, (kv, kv_across))
        )
        total = sum(jnp.sum(weight, axis=1, keepdims=True) for weight in p)
        for i, h in enumerate(heads):
            at = slice(i * rows, (i + 1) * rows)
            out[:, h * HD:(h + 1) * HD] = mixed[at].astype(BF)
            peaks.append(peak[at])
            totals.append(total[at])
    store_stats(out, slice(0, rows), peaks, totals)


def self_attention(info, ids, q, kv, kv_across, rows):
    return pl.pallas_call(
        self_kernel,
        out_shape=jax.ShapeDtypeStruct((rows, WIDTH), BF),
        in_specs=[SMEM] + [VMEM] * 4,
        out_specs=VMEM,
        compiler_params=params(10),
        cost_estimate=cost(5),
    )(info, ids, q, kv, kv_across)


def merge_kernel(count, final, info, *refs):
    parts, outs = refs[:count], refs[count:]
    rows = outs[0].shape[0]
    tile = min(rows, 64)
    lane = lax.broadcasted_iota(jnp.int32, (tile, HD), 1)
    for k, out in enumerate(outs):
        for start in range(0, rows, tile):
            if len(outs) == 4:
                first = pl.multiple_of(lax.rem(info[0] + k, 4) * rows, rows) + start
                at = pl.ds(pl.multiple_of(first, min(tile, 16)), tile)
            else:
                at = slice(k * rows + start, k * rows + start + tile)
            to = slice(start, start + tile)
            stats = [part[at, QH * HD:].astype(F32) for part in parts]
            top = functools.reduce(jnp.maximum, stats)
            weights = [jnp.exp2(jnp.where(lane < QH, stat - top, 0.0)) for stat in stats]
            totals = [pltpu.roll(stat, HD - 16, 1) + pltpu.roll(stat, HD - 32, 1) for stat in stats]
            total = sum(w * t for w, t in zip(weights, totals))
            if final:
                inverse = 1.0 / jnp.where(lane < QH, total, 1.0)
                weights = [w * inverse for w in weights]
            for h in range(QH):
                here = slice(h * HD, (h + 1) * HD)
                mixed = sum(
                    part[at, here].astype(F32) * w[:, h:h + 1] for part, w in zip(parts, weights)
                )
                out[to, here] = mixed.astype(BF)
            if not final:
                total = jnp.where(lane < QH, total, 0.0)
                top = jnp.where(lane < QH, top, 0.0)
                high = total.astype(BF).astype(F32)
                packed = top + pltpu.roll(high, 16, 1) + pltpu.roll(total - high, 32, 1)
                out[to, QH * HD:] = packed.astype(BF)


def merge(parts, count=1, turn=None, final=False):
    rows = parts[0].shape[0] // count
    turn = jnp.zeros((1,), jnp.int32) if turn is None else turn.reshape(1)
    shape = jax.ShapeDtypeStruct((rows, QH * HD if final else WIDTH), BF)
    return pl.pallas_call(
        functools.partial(merge_kernel, len(parts), final),
        out_shape=(shape,) * count,
        in_specs=[SMEM] + [VMEM] * len(parts),
        out_specs=(VMEM,) * count,
        compiler_params=params(10),
        cost_estimate=cost(0.3 * sum(part.shape[0] for part in parts) / 128),
    )(turn, *parts)


def join_kernel(*refs):
    to = 0
    for ref in refs[:-1]:
        refs[-1][to:to + ref.shape[0], :] = ref[...]
        to += ref.shape[0]


def join(*arrays):
    return pl.pallas_call(
        join_kernel,
        out_shape=jax.ShapeDtypeStruct((sum(a.shape[0] for a in arrays), arrays[0].shape[1]), BF),
        in_specs=[VMEM] * len(arrays),
        out_specs=VMEM,
        compiler_params=params(10),
        cost_estimate=cost(0.02),
    )(*arrays)


def send_on(arrays, to):
    return [lax.ppermute(array, "seq", to(k)) for k, array in enumerate(arrays) if k]


def broadcast_stages(seq):
    l, x, z, c = coords(seq)
    return [
        (route_from(lambda l, x, z, c: (l, x, z, c) == (0, 0, 0, 0), lambda l, x, z, c: (l, x, 2, c)),
         (l == 0) & (x == 0) & (z == 2) & (c == 0)),
        (route_from(lambda l, x, z, c: l == 0 and x == 0 and z in (0, 2) and c == 0, lambda l, x, z, c: (l, x, z + 1, c)),
         (l == 0) & (x == 0) & (z % 2 == 1) & (c == 0)),
        (route_from(lambda l, x, z, c: l == 0 and x == 0 and c == 0, lambda l, x, z, c: (l, 2, z, c)),
         (l == 0) & (x == 2) & (c == 0)),
        (route_from(lambda l, x, z, c: l == 0 and x in (0, 2) and c == 0, lambda l, x, z, c: (l, x + 1, z, c)),
         (l == 0) & (x % 2 == 1) & (c == 0)),
        (route_from(lambda l, x, z, c: l == 0 and c == 0, lambda l, x, z, c: (1, x, z, c)),
         (l == 1) & (c == 0)),
        (route_from(lambda l, x, z, c: c == 0, lambda l, x, z, c: (l, x, z, 1)), c == 1),
    ]


def route_from(holds, move):
    return [(s, number(*move(*coords(s)))) for s in range(64) if holds(*coords(s))]


def turns(positions):
    exponent = jnp.arange(HD // 2, dtype=F32) * (-2.0 / HD)
    frequency = jnp.power(F32(rope_base), exponent)
    angles = positions.astype(F32)[:, None] * frequency[None, :]
    cos, sin = jnp.cos(angles), jnp.sin(angles)
    return jnp.concatenate([cos, cos], axis=1), jnp.concatenate([-sin, sin], axis=1)


def tie(*values):
    return lax.optimization_barrier(values)


def local(ctx_hidden, fin_hidden, lengths, ln_gain, q_weight, k_weight, v_weight, q_gain, k_gain):
    ctx_count, half = ctx_hidden.shape
    fin_count = fin_hidden.shape[0]
    head = lax.axis_index("head").astype(jnp.int32)
    seq = lax.axis_index("seq").astype(jnp.int32)
    axes = ("seq", "head")
    own_gain = ln_gain.reshape(1, half)
    high = lax.reduce_precision(own_gain, 8, 7)
    middle = lax.reduce_precision(own_gain - high, 8, 7)
    low = own_gain - high - middle
    pieces = [piece.astype(BF) for piece in (high, middle, low)]
    sent = jnp.concatenate([fin_hidden] + pieces + [jnp.zeros((13, half), BF)], axis=0)
    received = lax.ppermute(sent, "head", SWAP)
    near_own = lax.ppermute(fin_hidden, "seq", TO_Y)
    near_other = lax.ppermute(fin_hidden, axes, TO_CROSS)
    split = ctx_count // 2
    soon = lax.ppermute(ctx_hidden[:split], "head", SWAP)
    ahead = lax.ppermute(ctx_hidden[split:], axes, SWAP_FIRST)
    others = lax.ppermute(ctx_hidden[split:], axes, SWAP_REST)

    weights = (q_weight, k_weight, v_weight)
    block_ids = jnp.arange(64, dtype=jnp.int32)
    own_start = jnp.sum(jnp.where(block_ids < seq, lengths, 0))
    own_length = jnp.sum(jnp.where(block_ids == seq, lengths, 0))
    live_total = jnp.sum(lengths)
    my_l, my_x, my_z, my_c = coords(seq)
    near = number(1 - my_l, my_x, my_z, my_c)
    fin_ids = jnp.arange(fin_count, dtype=jnp.int32)
    fin_positions = live_total + jnp.concatenate([seq * fin_count + fin_ids, near * fin_count + fin_ids])

    info = jnp.stack([seq, own_length, lengths[0], jnp.int32(fin_count)])
    other_gain = sum(received[fin_count + i:fin_count + i + 1].astype(F32) for i in range(3))
    shared = (
        jnp.stack([head, seq]), own_gain, other_gain, q_gain.reshape(1, HD), k_gain.reshape(1, HD), *weights,
    )
    own_qkv = fin_project(shared, turns(fin_positions), (fin_hidden, received, near_own, near_other))
    own_qkv, own_start = tie(own_qkv, own_start)
    turn = turns(own_start + jnp.arange(ctx_count, dtype=jnp.int32))
    def double(array, pairs):
        return lax.ppermute(array, "seq", pairs)

    passed = double(own_qkv, to_x(1))
    own_qkv, passed, turn = tie(own_qkv, passed, turn)
    gathered = join(own_qkv, passed)
    gathered = join(gathered, double(gathered, to_x(2)))
    passed = double(gathered, to_z(1))
    gathered, soon = tie(gathered, soon)
    kv_soon, normed = kv_project(shared, turn, ctx_hidden, ((soon, 0),), 0, split)
    passed, kv_soon = tie(passed, kv_soon)
    gathered = join(gathered, passed)
    passed = double(gathered, to_z(2))
    kv_soon, ahead = tie(kv_soon, ahead)
    kv_ahead = kv_project(shared, turn, ctx_hidden, ((ahead, 0),), split, split)[0]
    stages = broadcast_stages(seq)
    anchor = join(kv_soon, kv_ahead)

    def send(stage):
        return lax.ppermute(anchor, "seq", stages[stage][0])

    def take(stage):
        return jnp.where(stages[stage][1], arrived, anchor)

    arrived = send(0)
    anchor, normed = tie(anchor, normed)
    q_soon = project_queries(shared, turn, normed, 0, 0.1)
    q_soon, arrived, others, passed = tie(q_soon, arrived, others, passed)
    anchor = take(0)
    arrived = send(1)
    gathered = join(gathered, passed)
    across = lax.ppermute(gathered, "seq", TO_CORE)
    kv_late, normed = kv_project(
        shared, turn, ctx_hidden, ((others, 0), (ahead, 0)), split, split, room=58
    )
    kv_late, arrived, across = tie(kv_late, arrived, across)
    anchor = take(1)
    arrived = send(2)
    kv = join(kv_soon, kv_late)
    away = fin_attention(0, info, across, [kv])
    passed = lax.ppermute(away, "seq", TO_CORE)
    part = fin_attention(0, info, gathered, [kv])
    part, passed, normed = tie(part, passed, normed)
    partial = merge([part, passed], 4)
    passed = send_on(partial, to_z)
    partial, normed, arrived = tie(partial, normed, arrived)
    anchor = take(2)
    arrived = send(3)
    q_late = project_queries(shared, turn, normed, split)
    q_late, arrived = tie(q_late, arrived)
    anchor = take(3)
    arrived = send(4)
    slot = jnp.arange(64, dtype=jnp.int32)
    owner = number(my_l ^ (slot % 2), my_x ^ (slot // 2 % 4), my_z ^ (slot // 8 % 4), my_c ^ (slot // 32))
    ids = (owner[:, None] * fin_count + fin_ids[None, :]).reshape(1, -1)
    own_part = self_attention(info, ids, own_qkv, gathered, across, fin_count)
    passed, own_part, arrived = tie(passed, own_part, arrived)
    anchor = take(4)
    partial = merge([partial[0]] + passed, 4)
    passed = send_on(partial, to_x)
    partial, anchor = tie(partial, anchor)
    arrived = send(5)
    anchor = take(5)
    ctx_out = ctx_attention(0, split, info, q_soon, anchor, kv, None)
    passed, ctx_out = tie(passed, ctx_out)
    partial = merge([partial[0]] + passed, 2)
    passed = lax.ppermute(partial[1], "seq", TO_Y)
    partial, ctx_out = tie(partial, ctx_out)
    ctx_out = ctx_attention(split, split, info, q_late, anchor, kv, ctx_out)
    passed, ctx_out = tie(passed, ctx_out)
    fin_out = merge([partial[0], passed, own_part], final=True)[0]
    return ctx_out, fin_out


def solution(mesh):
    return jax.shard_map(
        local,
        mesh=mesh,
        in_specs=(
            P("seq", "head"),
            P("seq", "head"),
            P(),
            P("head"),
            P(None, "head"),
            P(None, "head"),
            P(None, "head"),
            P(),
            P(),
        ),
        out_specs=(P("seq", "head"), P("seq", "head")),
        check_vma=False,
    )
```

```python
import functools

import jax
import jax.numpy as jnp
from jax import lax
from jax.experimental import pallas as pl
from jax.experimental.pallas import tpu as pltpu
from jax.sharding import PartitionSpec as P

HD = 128
GROUP = 5
KVH = 2
QH = 10
eps_norm = 1e-06
rope_base = 1000000.0
masked_score = -1e30
log2e = 1.4426950408889634
score_factor = HD ** (-0.5) * log2e
CHUNK = 128
F32 = jnp.float32
BF = jnp.bfloat16
NT = (((1,), (1,)), ((), ()))
SWAP = [(0, 1), (1, 0)]


def number(l, x, z, c):
    return ((l * 4 + x) * 4 + z) * 2 + c


def coords(s):
    return s // 32, s // 8 % 4, s // 2 % 4, s % 2


def route(move):
    return [(s, number(*move(*coords(s)))) for s in range(64)]


def to_z(k):
    return route(lambda l, x, z, c: (l, x, z ^ k, c))


def to_x(k):
    return route(lambda l, x, z, c: (l, x ^ k, z, c))


def both(move):
    pairs = []
    for s in range(64):
        l, x, z, c = coords(s)
        for h in range(2):
            to_l, to_h = move(l, h)
            pairs.append((2 * s + h, 2 * number(to_l, x, z, c) + to_h))
    return pairs


TO_CROSS = both(lambda l, h: (1 - l, 1 - h))
SWAP_FIRST = [(0, 1), (1, 0)]
SWAP_REST = [pair for pair in both(lambda l, h: (l, 1 - h)) if pair[0] > 1]
TO_Y = route(lambda l, x, z, c: (1 - l, x, z, c))
TO_CORE = route(lambda l, x, z, c: (l, x, z, 1 - c))


VMEM = pl.BlockSpec(memory_space=pltpu.VMEM)
SMEM = pl.BlockSpec(memory_space=pltpu.SMEM)
ANY = pl.BlockSpec(memory_space=pl.ANY)
WIDTH = (QH + 1) * HD


def cost(time):
    return pl.CostEstimate(
        flops=int(time * 1.15e9), bytes_accessed=int(time * 1e6), transcendentals=0
    )


def params(megabytes):
    return pltpu.CompilerParams(vmem_limit_bytes=megabytes << 20)


def normalize(own, others, gain_own, gain_other, place, normed, to, rows):
    half = own.shape[1]
    mine = pl.multiple_of(place[0] * half, half)
    theirs = pl.multiple_of((1 - place[0]) * half, half)

    def run(other):
        @pl.loop(0, rows // 16)
        def _(step):
            at = pl.ds(pl.multiple_of(step * 16, 16), 16)
            put = pl.ds(pl.multiple_of(step * 16 + to, 16), 16)
            a = own[at, :].astype(F32)
            b = other[at, :].astype(F32)
            total = jnp.sum(a * a + b * b, axis=1, keepdims=True)
            scale = lax.rsqrt(total / (2 * half) + eps_norm)
            normed[put, pl.ds(mine, half)] = (a * scale * gain_own[...]).astype(BF)
            normed[put, pl.ds(theirs, half)] = (b * scale * gain_other[...]).astype(BF)

    for use, other in others:
        if use is None:
            run(other)
        else:
            pl.when(use)(functools.partial(run, other))


def fin_project_kernel(
    place, own, other, near_own, near_other, gain_own, gain_other, q_gain, k_gain, cos, sin, wq, wk, wv,
    out, normed, weights, sems,
):
    copies = []
    for n in range(7):
        source = wq.at[:, pl.ds(n * 256, 256)] if n < 5 else (wk if n == 5 else wv)
        copies.append(pltpu.make_async_copy(source, weights.at[n], sems.at[n]))
        copies[-1].start()
    rows = own.shape[0]
    normalize(own, [(None, other)], gain_own, gain_other, place, normed, 0, rows)
    normalize(near_own, [(None, near_other)], gain_own, gain_other, place, normed, rows, rows)
    for n in range(7):
        copies[n].wait()
        gain = q_gain if n < 5 else k_gain
        project_columns(n, normed[...], weights[n], gain, cos, sin, out, out, QH * HD)


def fin_project(shared, turn, arrays):
    place, gain_own, gain_other, q_gain, k_gain, *weights = shared
    rows = 2 * arrays[0].shape[0]
    return pl.pallas_call(
        fin_project_kernel,
        out_shape=jax.ShapeDtypeStruct((rows, (QH + 2 * KVH) * HD), BF),
        in_specs=[SMEM] + [VMEM] * 10 + [ANY] * 3,
        out_specs=VMEM,
        scratch_shapes=[
            pltpu.VMEM((rows, 5120), BF),
            pltpu.VMEM((7, 5120, 256), BF),
            pltpu.SemaphoreType.DMA((7,)),
        ],
        compiler_params=params(52),
        cost_estimate=cost(0.1),
    )(place, *arrays, gain_own, gain_other, q_gain, k_gain, *turn, *weights)


def kv_kernel(
    count, place, gain_own, gain_other, k_gain, own, *rest,
):
    others, (cos, sin, wk, wv, kv_out, normed, weights, sems) = rest[:count], rest[count:]
    copies = [pltpu.make_async_copy(w, weights.at[i], sems.at[i]) for i, w in enumerate((wk, wv))]

    @pl.when(pl.program_id(0) == 0)
    def _():
        for copy in copies:
            copy.start()

    uses = [(None, others[0])]
    if count == 2:
        uses = [(place[1] != 0, others[0]), (place[1] == 0, others[1])]
    normalize(own, uses, gain_own, gain_other, place, normed, 0, own.shape[0])

    @pl.when(pl.program_id(0) == 0)
    def _():
        for copy in copies:
            copy.wait()

    for i in range(2):
        project_columns(5 + i, normed[...], weights[i], k_gain, cos, sin, None, kv_out, 0)


def kv_project(shared, turn, own, others, first, rows, room=40):
    place, gain_own, gain_other, _, k_gain, _, wk, wv = shared
    half = own.shape[1]
    tile = 128
    whole = lambda array: pl.BlockSpec(array.shape, lambda i: (0, 0))
    tiles = lambda width: pl.BlockSpec((tile, width), lambda i: (i, 0))
    from_row = lambda start, width: pl.BlockSpec((tile, width), lambda i: (i + start // tile, 0))
    later = functools.partial(from_row, first)
    return pl.pallas_call(
        functools.partial(kv_kernel, len(others)),
        grid=(rows // tile,),
        out_shape=(
            jax.ShapeDtypeStruct((rows, 2 * KVH * HD), BF),
            jax.ShapeDtypeStruct((rows, 2 * half), BF),
        ),
        in_specs=[SMEM, whole(gain_own), whole(gain_other), whole(k_gain)]
        + [later(half)] + [from_row(start, half) for _, start in others] + [later(HD)] * 2 + [ANY] * 2,
        out_specs=(tiles(2 * KVH * HD), tiles(2 * half)),
        scratch_shapes=[pltpu.VMEM((2, 2 * half, 256), BF), pltpu.SemaphoreType.DMA((2,))],
        compiler_params=params(room),
        cost_estimate=cost(0.02 * rows / 128),
    )(place, gain_own, gain_other, k_gain, own, *[array for array, _ in others], *turn, wk, wv)


def project_columns(n, normed, weight, gain, cos, sin, q_out, kv_out, shift):
    raw = jnp.dot(normed, weight, preferred_element_type=F32)
    for part in range(2):
        piece = raw[:, part * HD:(part + 1) * HD]
        if n == 6:
            kv_out[:, shift + (KVH + part) * HD:shift + (KVH + part + 1) * HD] = piece.astype(BF)
            continue
        mean = jnp.sum(piece * piece, axis=1, keepdims=True) * (1.0 / HD)
        piece = piece * lax.rsqrt(mean + eps_norm) * gain[...]
        turned = pltpu.roll(piece, HD // 2, 1)
        piece = (piece * cos[...] + turned * sin[...]).astype(BF)
        if n < 5:
            q_out[:, n * 256 + part * HD:n * 256 + (part + 1) * HD] = piece
        else:
            kv_out[:, shift + part * HD:shift + (part + 1) * HD] = piece


def queries_kernel(q_gain, cos, sin, wq, normed, out):
    project_columns(0, normed[...], wq[...], q_gain, cos, sin, out, None, 0)


def project_queries(shared, turn, normed, first, time=8):
    q_gain, wq = shared[3], shared[5]
    rows, depth = normed.shape
    whole = lambda array: pl.BlockSpec(array.shape, lambda i: (0, 0))
    turned = pl.BlockSpec((rows, HD), lambda i: (first // rows, 0))
    return pl.pallas_call(
        queries_kernel,
        grid=(5,),
        out_shape=jax.ShapeDtypeStruct((rows, QH * HD), BF),
        in_specs=[whole(q_gain), turned, turned, pl.BlockSpec((depth, 256), lambda i: (0, i)), whole(normed)],
        out_specs=pl.BlockSpec((rows, 256), lambda i: (0, i)),
        compiler_params=params(40),
        cost_estimate=cost(time),
    )(q_gain, *turn, wq, normed)


def guard(kv, count, keys, values):
    rows = kv.shape[0]
    live = lax.broadcasted_iota(jnp.int32, (rows, HD), 0) < count
    ones = jnp.where(live, 1.0, 0.0).astype(BF)
    for g in range(KVH):
        key = kv[:, g * HD:(g + 1) * HD].astype(F32)
        keys[:, g * HD:(g + 1) * HD] = jnp.where(live, key, key[0:1, :]).astype(BF)
        value = kv[:, (KVH + g) * HD:(KVH + g + 1) * HD].astype(F32)
        values[:, 2 * g * HD:(2 * g + 1) * HD] = jnp.where(live, value, 0.0).astype(BF)
        values[:, (2 * g + 1) * HD:(2 * g + 2) * HD] = ones


def ctx_kernel(first, info, anchor, q, kv, *refs):
    out, keys, values, own_keys, own_values = refs[-5:]
    position, own_length, anchor_length = info[0], info[1], info[2]
    guard(anchor, jnp.where(position > 0, anchor_length, 0), keys, values)
    own_keys[...] = kv[:, :KVH * HD]
    for g in range(KVH):
        own_values[:, 2 * g * HD:(2 * g + 1) * HD] = kv[:, (KVH + g) * HD:(KVH + g + 1) * HD]
        own_values[:, (2 * g + 1) * HD:(2 * g + 2) * HD] = jnp.ones((kv.shape[0], HD), BF)
    tile = 128
    row = lax.broadcasted_iota(jnp.int32, (tile, HD), 0)
    causal = lax.broadcasted_iota(jnp.int32, (tile, tile), 1) <= lax.broadcasted_iota(
        jnp.int32, (tile, tile), 0
    )
    for start in range(0, out.shape[0], tile):
        before = first + start
        at = put = slice(start, start + tile)
        live = row + before < own_length
        for h in range(QH):
            g = h // GROUP
            here, there = slice(h * HD, (h + 1) * HD), slice(g * HD, (g + 1) * HD)
            both_columns = slice(2 * g * HD, (2 * g + 2) * HD)
            query = q[at, here]
            scores = [lax.dot_general(query, keys[:, there], NT, preferred_element_type=F32)]
            if before:
                scores.append(
                    lax.dot_general(query, own_keys[:before, there], NT, preferred_element_type=F32)
                )
            last = lax.dot_general(
                query, own_keys[before:before + tile, there], NT, preferred_element_type=F32
            )
            scores.append(jnp.where(causal, last, masked_score))
            peak = functools.reduce(
                jnp.maximum, [jnp.max(score, axis=1, keepdims=True) for score in scores]
            ) * score_factor
            p = [jnp.exp2(score * score_factor - peak).astype(BF) for score in scores]
            mixed = jnp.dot(p[0], values[:, both_columns], preferred_element_type=F32)
            if before:
                mixed += jnp.dot(p[1], own_values[:before, both_columns], preferred_element_type=F32)
            mixed += jnp.dot(
                p[-1], own_values[before:before + tile, both_columns], preferred_element_type=F32
            )
            result = mixed[:, :HD] / mixed[:, HD:]
            out[put, here] = jnp.where(live, result, 0.0).astype(BF)


def ctx_attention(first, rows, info, q, anchor, kv, base):
    count = kv.shape[0]
    extra = [] if base is None else [base]
    return pl.pallas_call(
        functools.partial(ctx_kernel, first),
        grid=(1,),
        out_shape=jax.ShapeDtypeStruct((count, QH * HD), BF),
        in_specs=[SMEM] + [VMEM] * 3 + [pl.BlockSpec(memory_space=pl.ANY)] * len(extra),
        out_specs=pl.BlockSpec((rows, QH * HD), lambda i: (first // rows, 0)),
        scratch_shapes=[
            pltpu.VMEM((count, KVH * HD), BF),
            pltpu.VMEM((count, 2 * KVH * HD), BF),
            pltpu.VMEM((count, KVH * HD), BF),
            pltpu.VMEM((count, 2 * KVH * HD), BF),
        ],
        input_output_aliases={4: 0} if extra else {},
        compiler_params=params(10),
        cost_estimate=cost(5),
    )(info, anchor, q, kv, *extra)


def store_stats(out, at, peaks, totals):
    lane = lax.broadcasted_iota(jnp.int32, (at.stop - at.start, HD), 1)
    peak, total = jnp.zeros(lane.shape, F32), jnp.zeros(lane.shape, F32)
    for h in range(QH):
        peak = jnp.where(lane == h, peaks[h], peak)
        total = jnp.where(lane == h, totals[h], total)
    high = total.astype(BF).astype(F32)
    stats = peak + pltpu.roll(high, 16, 1) + pltpu.roll(total - high, 32, 1)
    out[at, QH * HD:] = stats.astype(BF)


def fin_kernel(first, count, info, q, *refs):
    kvs = refs[:count]
    out, keys, values, joined = refs[count:]
    own_length = info[1]
    to = 0
    for kv in kvs:
        joined[to:to + kv.shape[0], :] = kv[...]
        to += kv.shape[0]
    guard(joined, own_length - first, keys, values)
    floor = jnp.where(own_length > first, 0.0, masked_score)
    tile = 256
    for start in range(0, q.shape[0], tile):
        at = slice(start, start + tile)
        peaks, totals = [], []
        for h in range(QH):
            g = h // GROUP
            here, there = slice(h * HD, (h + 1) * HD), slice(g * HD, (g + 1) * HD)
            score = lax.dot_general(q[at, here], keys[:, there], NT, preferred_element_type=F32)
            peak = (jnp.max(score, axis=1, keepdims=True) * score_factor).astype(BF).astype(F32)
            p = jnp.exp2(score * score_factor - peak).astype(BF)
            mixed = jnp.dot(p, values[:, 2 * g * HD:(2 * g + 2) * HD], preferred_element_type=F32)
            out[at, here] = mixed[:, :HD].astype(BF)
            peaks.append(peak + floor)
            totals.append(mixed[:, HD:])
        store_stats(out, at, peaks, totals)


def fin_attention(first, info, q, kvs):
    rows, keys = q.shape[0], sum(kv.shape[0] for kv in kvs)
    return pl.pallas_call(
        functools.partial(fin_kernel, first, len(kvs)),
        out_shape=jax.ShapeDtypeStruct((rows, WIDTH), BF),
        in_specs=[SMEM] + [VMEM] * (1 + len(kvs)),
        out_specs=VMEM,
        scratch_shapes=[
            pltpu.VMEM((keys, KVH * HD), BF),
            pltpu.VMEM((keys, 2 * KVH * HD), BF),
            pltpu.VMEM((keys, 2 * KVH * HD), BF),
        ],
        compiler_params=params(10),
        cost_estimate=cost(5),
    )(info, q, *kvs)


def self_kernel(info, ids, q, kv, kv_across, out):
    rows = out.shape[0]
    shift = QH * HD
    tall = GROUP * rows
    queries = info[0] * rows + lax.rem(lax.broadcasted_iota(jnp.int32, (tall, 512), 0), rows)
    allowed = [ids[:, :512] <= queries, ids[:, 512:] <= queries]
    peaks, totals = [], []
    for g in range(KVH):
        heads = range(g * GROUP, (g + 1) * GROUP)
        query = jnp.concatenate([q[:rows, h * HD:(h + 1) * HD] for h in heads], axis=0)
        there = slice(shift + g * HD, shift + (g + 1) * HD)
        value = slice(shift + (KVH + g) * HD, shift + (KVH + g + 1) * HD)
        scores = [
            jnp.where(
                mask, lax.dot_general(query, part[:, there], NT, preferred_element_type=F32), masked_score
            )
            for mask, part in zip(allowed, (kv, kv_across))
        ]
        peak = jnp.maximum(*[jnp.max(score, axis=1, keepdims=True) for score in scores])
        peak = (peak * score_factor).astype(BF).astype(F32)
        p = [jnp.exp2(score * score_factor - peak) for score in scores]
        mixed = sum(
            jnp.dot(weight.astype(BF), part[:, value], preferred_element_type=F32)
            for weight, part in zip(p, (kv, kv_across))
        )
        total = sum(jnp.sum(weight, axis=1, keepdims=True) for weight in p)
        for i, h in enumerate(heads):
            at = slice(i * rows, (i + 1) * rows)
            out[:, h * HD:(h + 1) * HD] = mixed[at].astype(BF)
            peaks.append(peak[at])
            totals.append(total[at])
    store_stats(out, slice(0, rows), peaks, totals)


def self_attention(info, ids, q, kv, kv_across, rows):
    return pl.pallas_call(
        self_kernel,
        out_shape=jax.ShapeDtypeStruct((rows, WIDTH), BF),
        in_specs=[SMEM] + [VMEM] * 4,
        out_specs=VMEM,
        compiler_params=params(10),
        cost_estimate=cost(5),
    )(info, ids, q, kv, kv_across)


def merge_kernel(count, final, info, *refs):
    parts, outs = refs[:count], refs[count:]
    rows = outs[0].shape[0]
    tile = min(rows, 64)
    lane = lax.broadcasted_iota(jnp.int32, (tile, HD), 1)
    for k, out in enumerate(outs):
        for start in range(0, rows, tile):
            if len(outs) == 4:
                first = pl.multiple_of(lax.rem(info[0] + k, 4) * rows, rows) + start
                at = pl.ds(pl.multiple_of(first, min(tile, 16)), tile)
            else:
                at = slice(k * rows + start, k * rows + start + tile)
            to = slice(start, start + tile)
            stats = [part[at, QH * HD:].astype(F32) for part in parts]
            top = functools.reduce(jnp.maximum, stats)
            weights = [jnp.exp2(jnp.where(lane < QH, stat - top, 0.0)) for stat in stats]
            totals = [pltpu.roll(stat, HD - 16, 1) + pltpu.roll(stat, HD - 32, 1) for stat in stats]
            total = sum(w * t for w, t in zip(weights, totals))
            if final:
                inverse = 1.0 / jnp.where(lane < QH, total, 1.0)
                weights = [w * inverse for w in weights]
            for h in range(QH):
                here = slice(h * HD, (h + 1) * HD)
                mixed = sum(
                    part[at, here].astype(F32) * w[:, h:h + 1] for part, w in zip(parts, weights)
                )
                out[to, here] = mixed.astype(BF)
            if not final:
                total = jnp.where(lane < QH, total, 0.0)
                top = jnp.where(lane < QH, top, 0.0)
                high = total.astype(BF).astype(F32)
                packed = top + pltpu.roll(high, 16, 1) + pltpu.roll(total - high, 32, 1)
                out[to, QH * HD:] = packed.astype(BF)


def merge(parts, count=1, turn=None, final=False):
    rows = parts[0].shape[0] // count
    turn = jnp.zeros((1,), jnp.int32) if turn is None else turn.reshape(1)
    shape = jax.ShapeDtypeStruct((rows, QH * HD if final else WIDTH), BF)
    return pl.pallas_call(
        functools.partial(merge_kernel, len(parts), final),
        out_shape=(shape,) * count,
        in_specs=[SMEM] + [VMEM] * len(parts),
        out_specs=(VMEM,) * count,
        compiler_params=params(10),
        cost_estimate=cost(0.3 * sum(part.shape[0] for part in parts) / 128),
    )(turn, *parts)


def join_kernel(*refs):
    to = 0
    for ref in refs[:-1]:
        refs[-1][to:to + ref.shape[0], :] = ref[...]
        to += ref.shape[0]


def join(*arrays):
    return pl.pallas_call(
        join_kernel,
        out_shape=jax.ShapeDtypeStruct((sum(a.shape[0] for a in arrays), arrays[0].shape[1]), BF),
        in_specs=[VMEM] * len(arrays),
        out_specs=VMEM,
        compiler_params=params(10),
        cost_estimate=cost(0.02),
    )(*arrays)


def send_on(arrays, to):
    return [lax.ppermute(array, "seq", to(k)) for k, array in enumerate(arrays) if k]


def broadcast_stages(seq):
    l, x, z, c = coords(seq)
    return [
        (route_from(lambda l, x, z, c: (l, x, z, c) == (0, 0, 0, 0), lambda l, x, z, c: (l, x, 2, c)),
         (l == 0) & (x == 0) & (z == 2) & (c == 0)),
        (route_from(lambda l, x, z, c: l == 0 and x == 0 and z in (0, 2) and c == 0, lambda l, x, z, c: (l, x, z + 1, c)),
         (l == 0) & (x == 0) & (z % 2 == 1) & (c == 0)),
        (route_from(lambda l, x, z, c: l == 0 and x == 0 and c == 0, lambda l, x, z, c: (l, 2, z, c)),
         (l == 0) & (x == 2) & (c == 0)),
        (route_from(lambda l, x, z, c: l == 0 and x in (0, 2) and c == 0, lambda l, x, z, c: (l, x + 1, z, c)),
         (l == 0) & (x % 2 == 1) & (c == 0)),
        (route_from(lambda l, x, z, c: l == 0 and c == 0, lambda l, x, z, c: (1, x, z, c)),
         (l == 1) & (c == 0)),
        (route_from(lambda l, x, z, c: c == 0, lambda l, x, z, c: (l, x, z, 1)), c == 1),
    ]


def route_from(holds, move):
    return [(s, number(*move(*coords(s)))) for s in range(64) if holds(*coords(s))]


def turns(positions):
    exponent = jnp.arange(HD // 2, dtype=F32) * (-2.0 / HD)
    frequency = jnp.power(F32(rope_base), exponent)
    angles = positions.astype(F32)[:, None] * frequency[None, :]
    cos, sin = jnp.cos(angles), jnp.sin(angles)
    return jnp.concatenate([cos, cos], axis=1), jnp.concatenate([-sin, sin], axis=1)


def tie(*values):
    return lax.optimization_barrier(values)


def local(ctx_hidden, fin_hidden, lengths, ln_gain, q_weight, k_weight, v_weight, q_gain, k_gain):
    ctx_count, half = ctx_hidden.shape
    fin_count = fin_hidden.shape[0]
    head = lax.axis_index("head").astype(jnp.int32)
    seq = lax.axis_index("seq").astype(jnp.int32)
    axes = ("seq", "head")
    own_gain = ln_gain.reshape(1, half)
    high = lax.reduce_precision(own_gain, 8, 7)
    middle = lax.reduce_precision(own_gain - high, 8, 7)
    low = own_gain - high - middle
    pieces = [piece.astype(BF) for piece in (high, middle, low)]
    sent = jnp.concatenate([fin_hidden] + pieces + [jnp.zeros((13, half), BF)], axis=0)
    received = lax.ppermute(sent, "head", SWAP)
    near_own = lax.ppermute(fin_hidden, "seq", TO_Y)
    near_other = lax.ppermute(fin_hidden, axes, TO_CROSS)
    split = ctx_count // 2
    soon = lax.ppermute(ctx_hidden[:split], "head", SWAP)
    ahead = lax.ppermute(ctx_hidden[split:], axes, SWAP_FIRST)
    others = lax.ppermute(ctx_hidden[split:], axes, SWAP_REST)

    weights = (q_weight, k_weight, v_weight)
    block_ids = jnp.arange(64, dtype=jnp.int32)
    own_start = jnp.sum(jnp.where(block_ids < seq, lengths, 0))
    own_length = jnp.sum(jnp.where(block_ids == seq, lengths, 0))
    live_total = jnp.sum(lengths)
    my_l, my_x, my_z, my_c = coords(seq)
    near = number(1 - my_l, my_x, my_z, my_c)
    fin_ids = jnp.arange(fin_count, dtype=jnp.int32)
    fin_positions = live_total + jnp.concatenate([seq * fin_count + fin_ids, near * fin_count + fin_ids])

    info = jnp.stack([seq, own_length, lengths[0], jnp.int32(fin_count)])
    other_gain = sum(received[fin_count + i:fin_count + i + 1].astype(F32) for i in range(3))
    shared = (
        jnp.stack([head, seq]), own_gain, other_gain, q_gain.reshape(1, HD), k_gain.reshape(1, HD), *weights,
    )
    own_qkv = fin_project(shared, turns(fin_positions), (fin_hidden, received, near_own, near_other))
    own_qkv, own_start = tie(own_qkv, own_start)
    turn = turns(own_start + jnp.arange(ctx_count, dtype=jnp.int32))
    def double(array, pairs):
        return lax.ppermute(array, "seq", pairs)

    passed = double(own_qkv, to_x(1))
    own_qkv, passed, turn = tie(own_qkv, passed, turn)
    gathered = join(own_qkv, passed)
    gathered = join(gathered, double(gathered, to_x(2)))
    passed = double(gathered, to_z(1))
    gathered, soon = tie(gathered, soon)
    kv_soon, normed = kv_project(shared, turn, ctx_hidden, ((soon, 0),), 0, split)
    passed, kv_soon = tie(passed, kv_soon)
    gathered = join(gathered, passed)
    passed = double(gathered, to_z(2))
    kv_soon, ahead = tie(kv_soon, ahead)
    kv_ahead = kv_project(shared, turn, ctx_hidden, ((ahead, 0),), split, split)[0]
    stages = broadcast_stages(seq)
    anchor = join(kv_soon, kv_ahead)

    def send(stage):
        return lax.ppermute(anchor, "seq", stages[stage][0])

    def take(stage):
        return jnp.where(stages[stage][1], arrived, anchor)

    arrived = send(0)
    anchor, normed = tie(anchor, normed)
    q_soon = project_queries(shared, turn, normed, 0, 0.1)
    q_soon, arrived, others, passed = tie(q_soon, arrived, others, passed)
    anchor = take(0)
    arrived = send(1)
    gathered = join(gathered, passed)
    across = lax.ppermute(gathered, "seq", TO_CORE)
    kv_late, normed = kv_project(
        shared, turn, ctx_hidden, ((others, 0), (ahead, 0)), split, split, room=58
    )
    kv_late, arrived, across = tie(kv_late, arrived, across)
    anchor = take(1)
    arrived = send(2)
    kv = join(kv_soon, kv_late)
    away = fin_attention(0, info, across, [kv])
    passed = lax.ppermute(away, "seq", TO_CORE)
    part = fin_attention(0, info, gathered, [kv])
    part, passed, normed = tie(part, passed, normed)
    partial = merge([part, passed], 4)
    passed = send_on(partial, to_z)
    partial, normed, arrived = tie(partial, normed, arrived)
    anchor = take(2)
    arrived = send(3)
    q_late = project_queries(shared, turn, normed, split)
    q_late, arrived = tie(q_late, arrived)
    anchor = take(3)
    arrived = send(4)
    slot = jnp.arange(64, dtype=jnp.int32)
    owner = number(my_l ^ (slot % 2), my_x ^ (slot // 2 % 4), my_z ^ (slot // 8 % 4), my_c ^ (slot // 32))
    ids = (owner[:, None] * fin_count + fin_ids[None, :]).reshape(1, -1)
    own_part = self_attention(info, ids, own_qkv, gathered, across, fin_count)
    passed, own_part = tie(passed, own_part)
    partial = merge([partial[0]] + passed, 4)
    passed = send_on(partial, to_x)
    partial, arrived = tie(partial, arrived)
    anchor = take(4)
    arrived = send(5)
    anchor = take(5)
    ctx_out = ctx_attention(0, split, info, q_soon, anchor, kv, None)
    passed, ctx_out = tie(passed, ctx_out)
    partial = merge([partial[0]] + passed, 2)
    passed = lax.ppermute(partial[1], "seq", TO_Y)
    partial, ctx_out = tie(partial, ctx_out)
    ctx_out = ctx_attention(split, split, info, q_late, anchor, kv, ctx_out)
    passed, ctx_out = tie(passed, ctx_out)
    fin_out = merge([partial[0], passed, own_part], final=True)[0]
    return ctx_out, fin_out


def solution(mesh):
    return jax.shard_map(
        local,
        mesh=mesh,
        in_specs=(
            P("seq", "head"),
            P("seq", "head"),
            P(),
            P("head"),
            P(None, "head"),
            P(None, "head"),
            P(None, "head"),
            P(),
            P(),
        ),
        out_specs=(P("seq", "head"), P("seq", "head")),
        check_vma=False,
    )
```
